128 devices in a mesh: leaf: 16 (over x, z), blk: 8 (over y, core).
Axes of the slice: x: 4, y: 4, z: 4, core: 2. Of those that a mesh axis runs over, the one named last changes fastest.
Arguments:
- particular: float32 [64, 73728], P('blk', 'leaf'), may hold values from -6 to 6
- root_inverse: float32 [12288, 12288], P('leaf', 'blk'), may hold values from -0.0390625 to 0.0390625
- mid_inverse: float32 [8192, 4096], P('leaf', 'blk'), may hold values from -0.0625 to 0.0625
- low_inverse: float32 [16384, 4096], P('leaf', 'blk'), may hold values from -0.0625 to 0.0625
- mid_lift: float32 [24576, 4096], P('leaf', 'blk'), may hold values from -0.0625 to 0.0625
- low_lift: float32 [40960, 4096], P('leaf', 'blk'), may hold values from -0.0625 to 0.0625
- mid_solve: float32 [8192, 12288], P('leaf', 'blk'), may hold values from -0.0546875 to 0.0546875
- low_solve: float32 [16384, 10240], P('leaf', 'blk'), may hold values from -0.0625 to 0.0625
Outputs:
- root_values: float32 [64, 12288], P('blk', 'leaf')
- middle_values: float32 [64, 8192], P('blk', 'leaf')
- lower_values: float32 [64, 16384], P('blk', 'leaf')
The draws below stay inside these ranges and needn't reach their ends.
All inputs are finite; a program needn't handle non-finite values.
Results may differ from the reference program's by a relative error of at most 0.00019.
Values sent between devices are 32-bit elements; how exact they have to be, the bound alone decides.
No kernel may reach another device: no remote copies, remote signals or barrier semaphores. Data moves between devices by JAX's collectives and lax.ppermute only.
A program may use at most 128 MiB of HBM per device.

```python
import jax
import jax.numpy as jnp
from jax import lax

IF0 = 12288
IF1 = 4096
IF2 = 4096
RHS = 64
BD1 = 12288
BD2 = 10240
BD3 = 9216


def block_levels(key, dims, pieces, low, top_value):
    loudness, own = 1.0, jax.random.fold_in(key, 6)
    for position, blocks in pieces:
        steps = jnp.exp(jax.random.uniform(jax.random.fold_in(own, position), (blocks,), jnp.float32, low / len(pieces), top_value / len(pieces)))
        loudness = loudness * jnp.repeat(steps, dims[position] // blocks).reshape([-1 if axis == position else 1 for axis in range(len(dims))])
    return loudness


def noise(rng, shape, deviation, most, shards=(), dtype=jnp.bfloat16):
    entries = deviation * jax.random.normal(rng, shape, jnp.float32)
    if shards:
        entries = entries * block_levels(rng, shape, shards, -0.22, 0.18)
    return jnp.clip(entries, -most, most).astype(dtype)


def setup_inputs(seed: int = 0) -> dict:
    streams_of = jax.random.split(jax.random.key(seed), 9)
    return {
        "particular": noise(streams_of[0], (RHS, 8 * BD3), 1.0, 6.0, ((0, 8), (1, 16)), jnp.float32),
        "root_inverse": noise(streams_of[1], (IF0, IF0), (2 * IF0) ** -0.5, 0.0390625, ((0, 16), (1, 8)), jnp.float32),
        "mid_inverse": noise(streams_of[2], (2 * IF1, IF1), (2 * IF1) ** -0.5, 0.0625, ((0, 16), (1, 8)), jnp.float32),
        "low_inverse": noise(streams_of[3], (4 * IF2, IF2), (2 * IF2) ** -0.5, 0.0625, ((0, 16), (1, 8)), jnp.float32),
        "mid_lift": noise(streams_of[4], (2 * BD1, IF1), (2 * IF1) ** -0.5, 0.0625, ((0, 16), (1, 8)), jnp.float32),
        "low_lift": noise(streams_of[5], (4 * BD2, IF2), (2 * IF2) ** -0.5, 0.0625, ((0, 16), (1, 8)), jnp.float32),
        "mid_solve": noise(streams_of[6], (2 * IF1, BD1), BD1 ** -0.5, 0.0546875, ((0, 16), (1, 8)), jnp.float32),
        "low_solve": noise(streams_of[7], (4 * IF2, BD2), BD2 ** -0.5, 0.0625, ((0, 16), (1, 8)), jnp.float32),
    }


def apply_op(vectors, operator):
    return jnp.dot(vectors, operator.T, precision=lax.Precision.HIGHEST, preferred_element_type=jnp.float32)


def merge_up(children, inverse_ops, lift_ops, count, child_size, half_size, iface, bound):
    weights = []
    fluxes = []
    for node_id in range(count):
        first_child = children[:, 2 * node_id * child_size:(2 * node_id + 1) * child_size]
        second_child = children[:, (2 * node_id + 1) * child_size:(2 * node_id + 2) * child_size]
        jump_vals = second_child[:, half_size:] - first_child[:, half_size:]
        weight_now = apply_op(jump_vals, inverse_ops[node_id * iface:(node_id + 1) * iface])
        outer_part = jnp.concatenate([first_child[:, :half_size], second_child[:, :half_size]], 1)
        flux_now = outer_part + apply_op(weight_now, lift_ops[node_id * bound:(node_id + 1) * bound])
        weights.append(weight_now)
        fluxes.append(flux_now)
    return weights, jnp.concatenate(fluxes, 1)


def reference(particular, root_inverse, mid_inverse, low_inverse, mid_lift, low_lift, mid_solve, low_solve):
    low_w, flux_two = merge_up(particular, low_inverse, low_lift, 4, BD3, BD2 // 2, IF2, BD2)
    mid_w, flux_one = merge_up(flux_two, mid_inverse, mid_lift, 2, BD2, BD1 // 2, IF1, BD1)
    half_one = BD1 // 2
    root_jump = flux_one[:, BD1:] - flux_one[:, :BD1]
    root_values = apply_op(root_jump, root_inverse)
    middle = []
    for node_id in range(2):
        middle.append(apply_op(root_values, mid_solve[node_id * IF1:(node_id + 1) * IF1]) + mid_w[node_id])
    lower = []
    for node_id in range(4):
        parent_id = node_id // 2
        side_id = node_id % 2
        bound_two = jnp.concatenate([root_values[:, side_id * half_one:(side_id + 1) * half_one], middle[parent_id]], 1)
        lower.append(apply_op(bound_two, low_solve[node_id * IF2:(node_id + 1) * IF2]) + low_w[node_id])
    return root_values, jnp.concatenate(middle, 1), jnp.concatenate(lower, 1)
```

```python
import jax
import jax.numpy as jnp
from jax import lax
from jax.sharding import PartitionSpec as P

AXES = ("leaf", "blk")
DEVICES = [(s // 32, s // 8 % 4, s // 2 % 4, s % 2) for s in range(128)]


def flat(x, z, y, c):
    return ((x * 4 + z) * 4 + y) * 2 + c


def send(value, hop):
    pairs = []
    for source, place in enumerate(DEVICES):
        target = hop(*place)
        if target is not None:
            pairs.append((source, flat(*target)))
    return lax.ppermute(value, AXES, pairs)


def exchange(value, key, order):
    groups = {}
    for source, place in enumerate(DEVICES):
        groups.setdefault(key(*place), []).append((order(*place), source))
    members = [[source for _, source in sorted(group)] for group in groups.values()]
    return lax.all_to_all(value, AXES, 0, 0, axis_index_groups=members)


def over_blk(value):
    return exchange(value, lambda x, z, y, c: (x, z), lambda x, z, y, c: 2 * y + c)


def over_leaf(value):
    return exchange(value, lambda x, z, y, c: (y, c), lambda x, z, y, c: 4 * x + z)


def over_half(value):
    return exchange(value, lambda x, z, y, c: (x // 2, y, c), lambda x, z, y, c: 4 * x + z)


def copies(value, number):
    return jnp.broadcast_to(value[None], (number, *value.shape))


def swap_core(value):
    return send(value, lambda x, z, y, c: (x, z, y, 1 - c))


def sum_y(value):
    return value + total([send(value, lambda x, z, y, c: (x, z, y ^ k, c)) for k in (1, 2, 3)])


def cols(value, start, size):
    return lax.dynamic_slice_in_dim(value, start, size, value.ndim - 1)


def rows(value, start, size):
    return lax.dynamic_slice_in_dim(value, start, size, 0)


def apply(vectors, operator):
    return lax.dot_general(
        vectors,
        operator,
        (((1,), (1,)), ((), ())),
        precision=lax.Precision.HIGH,
        preferred_element_type=jnp.float32,
    )


def pick(pieces, index):
    out = pieces[0]
    for number in range(1, len(pieces)):
        out = jnp.where(index == number, pieces[number], out)
    return out


def total(parts):
    out = parts[0]
    for part in parts[1:]:
        out = out + part
    return out


def widen(value):
    return value.transpose(0, 2, 1, 3).reshape(64, -1)


def local(
    particular, root_inverse, mid_inverse, low_inverse, mid_lift, low_lift, mid_solve, low_solve
):
    leaf, blk = lax.axis_index("leaf"), lax.axis_index("blk")
    x, z, y, c = leaf // 4, leaf % 4, blk // 2, blk % 2
    xh, xl = x // 2, x % 2

    inner = jnp.where(z == 3, 1.0, -1.0) * particular[:, 512:]
    inner = inner.reshape(8, 8, 512).transpose(1, 0, 2)
    spread = exchange(
        jnp.broadcast_to(inner[None], (4, 8, 8, 512)).reshape(32, 8, 512),
        lambda x, z, y, c: x,
        lambda x, z, y, c: (z, y, c),
    )
    jump_two = (spread[8:16] + spread[24:]).reshape(64, 512)

    low_part = apply(jump_two, low_inverse)
    half = cols(low_part, 512 * c, 512) + swap_core(cols(low_part, 512 * (1 - c), 512))
    low_w = send(sum_y(half), lambda x, z, y, c: (x, y, z, c))

    moved = send(
        particular[:, 2560:], lambda x, z, y, c: (x, z + 1, y, c) if z % 2 == 0 else None
    )
    outer = jnp.where(
        z % 2 == 0, particular[:, :2560], jnp.concatenate([moved, particular[:, :512]], 1)
    )
    mine = (jnp.arange(8) == blk)[:, None, None]
    flux_two = apply(low_w, low_lift) + jnp.where(mine, outer[None], 0.0).reshape(64, 2560)
    flux_two = flux_two + swap_core(flux_two)

    def holder(y, c):
        return 2 if 2 * y + c < 3 else 3

    def block(y):
        number = 2 * y + c
        return cols(flux_two, jnp.clip(6144 + 512 * number - 2560 * z, 0, 2048), 512)

    holds = z == jnp.where(blk < 3, 2, 3)
    parts = [jnp.where(holds, block(y), 0.0)]
    for k in (1, 2, 3):
        parts.append(
            send(
                block(y ^ k),
                lambda x, z, y, c: (x, z, y ^ k, c) if z == holder(y ^ k, c) else None,
            )
        )
    summed = jnp.where(xl == 1, 1.0, -1.0) * total(parts)
    summed = summed + send(
        summed, lambda x, z, y, c: (x ^ 1, z, y, c) if z == holder(y, c) else None
    )
    jump_one = total(
        [summed]
        + [
            send(summed, lambda x, z, y, c: (x, z ^ k, y, c) if z == holder(y, c) else None)
            for k in (1, 2, 3)
        ]
    )

    mid_part = apply(jump_one, mid_inverse)
    mid_sum = sum_y(mid_part + swap_core(mid_part))
    mid_w = send(
        mid_sum, lambda x, z, y, c: (x // 2 * 2 + c, y, x % 2 * 2 + z // 2, z % 2)
    )

    outer_half = lax.dynamic_index_in_dim(flux_two.reshape(4, 2, 8, 2560), c, 1, False)
    outer_half = outer_half.reshape(32, 2560)
    next_z = send(
        cols(outer_half, jnp.where(z == 0, 1024, jnp.where(z == 1, 512, 0)), 1536),
        lambda x, z, y, c: (x, z + 1, y, c) if z < 3 else None,
    )
    far_z = send(
        outer_half[:, 2048:], lambda x, z, y, c: (x, 3, y, c) if z == 1 else None
    )
    outer_one = pick(
        [
            outer_half[:, :1536],
            jnp.concatenate([next_z[:, 512:], outer_half[:, :512]], 1),
            next_z,
            jnp.concatenate([far_z, next_z[:, :1024]], 1),
        ],
        z,
    )

    lift_part = apply(mid_w, mid_lift).reshape(4, 2, 8, 1536)
    flux_one = lax.dynamic_index_in_dim(lift_part, c, 1, False) + swap_core(
        lax.dynamic_index_in_dim(lift_part, 1 - c, 1, False)
    )
    flux_one = jnp.where(xh == 1, 1.0, -1.0) * (flux_one + outer_one.reshape(4, 8, 1536))
    shares = flux_one.reshape(4, 8, 2, 768).transpose(2, 0, 1, 3).reshape(8, 8, 768)
    piece = total(
        list(exchange(shares, lambda x, z, y, c: (x % 2, z, c), lambda x, z, y, c: (x, y)))
    )
    every = over_leaf(copies(piece, 16))
    root_jump = widen(over_blk(every.reshape(2, 8, 8, 768).transpose(1, 0, 2, 3)))

    root_part = apply(root_jump, root_inverse)
    root_values = total(list(over_blk(root_part.reshape(8, 8, 768))))
    root_every = over_leaf(copies(root_values, 16))
    root_block = widen(over_blk(root_every.reshape(8, 2, 8, 768)))

    middle_part = apply(root_block, mid_solve) + mid_part
    middle_values = total(list(over_blk(middle_part.reshape(8, 8, 512))))
    middle_every = over_half(copies(middle_values, 8))

    root_half = lax.dynamic_slice_in_dim(root_every.reshape(2, 8, 8, 768), xl, 1, 0)[0]
    bound = jnp.concatenate(
        [
            root_half.transpose(1, 0, 2).reshape(8, 6144),
            middle_every.transpose(1, 0, 2).reshape(8, 4096),
        ],
        1,
    )
    bound = over_blk(bound.reshape(8, 8, 1280).transpose(1, 0, 2)).reshape(64, 1280)
    lower_part = low_part + apply(bound, low_solve)
    lower_values = total(list(over_blk(lower_part.reshape(8, 8, 1024))))
    return (root_values, middle_values, lower_values)


def solution(mesh):
    placed = (P("blk", "leaf"),) + (P("leaf", "blk"),) * 7
    return jax.shard_map(
        local,
        mesh=mesh,
        in_specs=placed,
        out_specs=(P("blk", "leaf"),) * 3,
        check_vma=False,
    )
```

```python
import jax
import jax.numpy as jnp
from jax import lax
from jax.experimental import pallas as pl
from jax.experimental.pallas import tpu as pltpu
from jax.sharding import PartitionSpec as P

AXES = ("leaf", "blk")
DEVICES = [(s // 32, s // 8 % 4, s // 2 % 4, s % 2) for s in range(128)]
ROWS = (((1,), (1,)), ((), ()))


def flat(x, z, y, c):
    return ((x * 4 + z) * 4 + y) * 2 + c


def send(value, hop):
    pairs = []
    for source, place in enumerate(DEVICES):
        target = hop(*place)
        if target is not None:
            pairs.append((source, flat(*target)))
    return lax.ppermute(value, AXES, pairs)


def exchange(value, key, order):
    groups = {}
    for source, place in enumerate(DEVICES):
        groups.setdefault(key(*place), []).append((order(*place), source))
    members = [[source for _, source in sorted(group)] for group in groups.values()]
    return lax.all_to_all(value, AXES, 0, 0, axis_index_groups=members)


def over_blk(value):
    return exchange(value, lambda x, z, y, c: (x, z), lambda x, z, y, c: 2 * y + c)


def over_leaf(value):
    return exchange(value, lambda x, z, y, c: (y, c), lambda x, z, y, c: 4 * x + z)


def over_half(value):
    return exchange(value, lambda x, z, y, c: (x // 2, y, c), lambda x, z, y, c: 4 * x + z)


def over_z(value):
    return exchange(value, lambda x, z, y, c: (x, y, c), lambda x, z, y, c: z)


def over_y(value):
    return exchange(value, lambda x, z, y, c: (x, z, c), lambda x, z, y, c: y)


def over_zy(value):
    return exchange(value, lambda x, z, y, c: (x, c), lambda x, z, y, c: 4 * z + y)


def over_sides(value):
    return exchange(value, lambda x, z, y, c: (x % 2, z), lambda x, z, y, c: (x, y, c))


def copies(value, number):
    return jnp.broadcast_to(value[None], (number, *value.shape))


def swap_core(value):
    return send(value, lambda x, z, y, c: (x, z, y, 1 - c))


def sum_y(value):
    return value + total([send(value, lambda x, z, y, c: (x, z, y ^ k, c)) for k in (1, 2, 3)])


def cols(value, start, size):
    return lax.dynamic_slice_in_dim(value, start, size, value.ndim - 1)


def pick(pieces, index):
    out = pieces[0]
    for number in range(1, len(pieces)):
        out = jnp.where(index == number, pieces[number], out)
    return out


def total(parts):
    out = parts[0]
    for part in parts[1:]:
        out = out + part
    return out


def place():
    leaf, blk = lax.axis_index("leaf"), lax.axis_index("blk")
    return leaf // 4, leaf % 4, blk // 2, blk % 2


def halves(value):
    high = value.astype(jnp.bfloat16)
    return high, (value - high.astype(jnp.float32)).astype(jnp.bfloat16)


def product(name, vectors, operator, inputs, outputs, store, tile, fetch=0):
    height, depth = operator.shape
    count, steps = len(inputs), height // tile

    def body(*refs):
        given, held, results = refs[:count], refs[count], refs[count + 1 :]
        moves = []
        if fetch:
            *results, room, sems = results
            for number in range(steps):
                here = pl.ds(number * tile, tile)
                moves.append(pltpu.make_async_copy(held.at[here], room.at[here], sems.at[number]))
                moves[-1].start()
            held = room
        high, low = halves(vectors(*given))
        both = jnp.concatenate([high, low], 0)
        for number in range(steps):
            if fetch:
                moves[number].wait()
            over, under = halves(held[number * tile : (number + 1) * tile, :])
            first = lax.dot_general(both, over, ROWS, preferred_element_type=jnp.float32)
            second = lax.dot_general(high, under, ROWS, preferred_element_type=jnp.float32)
            store(number, first[:64] + (first[64:] + second), *given, *results)

    block = pl.BlockSpec(memory_space=pltpu.VMEM)
    return pl.pallas_call(
        body,
        name=name,
        out_shape=[jax.ShapeDtypeStruct(shape, jnp.float32) for shape in outputs],
        in_specs=[block] * count + [pl.BlockSpec(memory_space=pl.ANY) if fetch else block],
        out_specs=[block] * len(outputs),
        scratch_shapes=[
            pltpu.VMEM((height, depth), jnp.float32),
            pltpu.SemaphoreType.DMA((steps,)),
        ]
        if fetch
        else [],
        compiler_params=pltpu.CompilerParams(vmem_limit_bytes=(fetch or 8) << 20),
        cost_estimate=pl.CostEstimate(
            flops=6 * 64 * height * depth, bytes_accessed=4 * height * depth, transcendentals=0
        ),
    )(*inputs, operator)


def gathered(parts, number):
    def body(parts, value, every):
        summed = total([parts[k] for k in range(parts.shape[0])])
        value[...] = summed
        for k in range(number):
            every[k] = summed

    shape = parts.shape[1:]
    return pl.pallas_call(
        body,
        name="gathered",
        out_shape=[
            jax.ShapeDtypeStruct(shape, jnp.float32),
            jax.ShapeDtypeStruct((number, *shape), jnp.float32),
        ],
        in_specs=[pl.BlockSpec(memory_space=pltpu.VMEM)],
        out_specs=[pl.BlockSpec(memory_space=pltpu.VMEM)] * 2,
        compiler_params=pltpu.CompilerParams(vmem_limit_bytes=8 << 20),
    )(parts)


def added(first, second, number=None):
    def body(first, second, out):
        if number is None:
            out[...] = first[...] + second[...]
        else:
            summed = first[...] + second[...]
            for k in range(number):
                out[k] = summed

    shape = first.shape if number is None else (number, *first.shape)
    return pl.pallas_call(
        body,
        name="added",
        out_shape=jax.ShapeDtypeStruct(shape, jnp.float32),
        in_specs=[pl.BlockSpec(memory_space=pltpu.VMEM)] * 2,
        out_specs=pl.BlockSpec(memory_space=pltpu.VMEM),
        compiler_params=pltpu.CompilerParams(vmem_limit_bytes=8 << 20),
    )(first, second)


def low_product(jump, operator):
    def vectors(jump):
        return (jump[4:8] + jump[12:16]).reshape(64, 512)

    def store(number, tile, jump, part, keep, give):
        part[:, 512 * number : 512 * (number + 1)] = tile
        core = place()[3]

        @pl.when(core == number)
        def _():
            keep[...] = tile

        @pl.when(core != number)
        def _():
            give[...] = tile

    shapes = [(64, 1024), (64, 512), (64, 512)]
    return product("low_w", vectors, operator, [jump], shapes, store, 512)


def lift_product(parts, particular, operator):
    def vectors(parts, particular):
        return parts[0] + parts[1] + (parts[2] + parts[3])

    def store(number, tile, parts, particular, keep, give, mine, other):
        x, z, y, c = place()
        if number == 0:
            keep[...] = jnp.zeros(keep.shape, jnp.float32)
            give[...] = jnp.zeros(give.shape, jnp.float32)
            for block in range(8):
                v, core = block // 2, block % 2
                source = 1024 + 512 * block if block < 7 else 0

                @pl.when((z == (2 if block < 7 else 3)) & (c == core))
                def _():
                    keep[y, v, pl.ds(pl.multiple_of(8 * c, 8), 8)] = particular[:, source : source + 512]

                @pl.when((z == (2 if block < 7 else 3)) & (c != core))
                def _():
                    give[y, v, pl.ds(pl.multiple_of(8 * c, 8), 8)] = particular[:, source : source + 512]

        here = pl.ds(512 * number, 512)
        block = number + jnp.where(z == 3, 3, -2)
        valid = (z == 3) | ((z == 2) & (number >= 2))
        row = jnp.clip(block // 2, 0, 3)

        @pl.when(valid & (block % 2 == c))
        def _():
            for k in range(4):
                keep[k, row] += tile[16 * k : 16 * k + 16]

        @pl.when(valid & (block % 2 != c))
        def _():
            for k in range(4):
                give[k, row] += tile[16 * k : 16 * k + 16]

        pairs = tile.reshape(4, 2, 8, 512)

        @pl.when(c == 0)
        def _():
            mine[:, :, here] = pairs[:, 0]
            other[:, :, here] = pairs[:, 1]

        @pl.when(c == 1)
        def _():
            mine[:, :, here] = pairs[:, 1]
            other[:, :, here] = pairs[:, 0]

    shapes = [(4, 4, 16, 512)] * 2 + [(4, 8, 2560)] * 2
    return product(
        "low_lift", vectors, operator, [parts, particular], shapes, store, 512
    )


def mid_product(parts, operator):
    def vectors(parts):
        return (parts[4:8] - parts[0:4]).reshape(64, 512)

    def store(number, tile, parts, out):
        out[:, 256 * number : 256 * (number + 1)] = tile

    return product("mid_w", vectors, operator, [parts], [(64, 512)], store, 256)[0]


def mid_lift_product(mid_w, outer, operator):
    def vectors(mid_w, outer):
        return mid_w[...]

    def store(number, tile, mid_w, outer, out):
        x, z, y, c = place()
        side, third = number // 3, number % 3
        added = outer[:, :, 256 * number : 256 * (number + 1)]
        sign = jnp.where(x // 2 == 1, 1.0, -1.0)
        pairs = tile.reshape(4, 2, 8, 256)
        for core in range(2):
            whole = sign * (pairs[:, core] + jnp.where(c == core, added, 0.0))
            for v in range(4):
                out[8 * side + 2 * v + core, :, 256 * third : 256 * (third + 1)] = whole[v]

    return product(
        "mid_lift", vectors, operator, [mid_w, outer], [(16, 8, 768)], store, 256
    )[0]


def wide_product(name, parts, operator, added=None):
    height = operator.shape[0]

    def vectors(parts, *added):
        return jnp.concatenate([parts[:, 0].reshape(64, 768), parts[:, 1].reshape(64, 768)], 1)

    def store(number, tile, *refs):
        here = slice(256 * number, 256 * (number + 1))
        if len(refs) == 3:
            tile = tile + refs[1][:, here]
        refs[-1][:, :, here] = tile.reshape(8, 8, 256)

    inputs = [parts] if added is None else [parts, added]
    return product(name, vectors, operator, inputs, [(8, 8, height)], store, 256)[0]


def last_product(bound, operator, added):
    def vectors(bound, added):
        return bound[...].reshape(64, 1280)

    def store(number, tile, bound, added, out):
        here = slice(256 * number, 256 * (number + 1))
        out[:, :, here] = (tile + added[:, here]).reshape(8, 8, 256)

    return product(
        "low_solve", vectors, operator, [bound, added], [(8, 8, 1024)], store, 256
    )[0]


def local(
    particular, root_inverse, mid_inverse, low_inverse, mid_lift, low_lift, mid_solve, low_solve
):
    x, z, y, c = place()
    xh, xl = x // 2, x % 2

    inner = (jnp.where(z == 3, 1.0, -1.0) * particular[:, 512:]).reshape(8, 4, 2, 512)
    keep = lax.dynamic_index_in_dim(inner, c, 2, False).transpose(1, 0, 2)
    got = swap_core(lax.dynamic_index_in_dim(inner, 1 - c, 2, False).transpose(1, 0, 2))
    both = jnp.concatenate([jnp.where(c == 0, keep, got), jnp.where(c == 0, got, keep)], 1)
    jump_two = over_zy(copies(both, 4).reshape(16, 16, 512))

    low_part, keep, give = low_product(jump_two, low_inverse)
    low_w = over_y(over_z(added(keep, swap_core(give), 4)))

    keep, give, mine, other = lift_product(low_w, particular, low_lift)

    blocks = added(keep, swap_core(give)).reshape(16, 16, 512)
    blocks, other, apart = lax.optimization_barrier((blocks, other, particular))
    jump_one = over_half(gathered(over_zy(blocks), 8)[1])

    mid_part = mid_product(jump_one, mid_inverse)
    mid_sum = sum_y(mid_part + swap_core(mid_part))
    mid_w = send(
        mid_sum, lambda x, z, y, c: (x // 2 * 2 + c, y ^ z, x % 2 * 2 + z // 2, z % 2)
    )

    moved = send(
        apart[:, 2560:], lambda x, z, y, c: (x, z + 1, y, c) if z % 2 == 0 else None
    )
    outer = jnp.where(
        z % 2 == 0, apart[:, :2560], jnp.concatenate([moved, apart[:, :512]], 1)
    )
    outer_half = mine + swap_core(other)
    outer_half = outer_half + jnp.where((jnp.arange(4) == y)[:, None, None], outer[None], 0.0)
    outer_half, mid_part = lax.optimization_barrier((outer_half, mid_part))
    next_z = send(
        cols(outer_half, jnp.where(z == 0, 1024, jnp.where(z == 1, 512, 0)), 1536),
        lambda x, z, y, c: (x, z + 1, y, c) if z < 3 else None,
    )
    far_z = send(
        outer_half[:, :, 2048:], lambda x, z, y, c: (x, 3, y, c) if z == 1 else None
    )
    outer_one = pick(
        [
            outer_half[:, :, :1536],
            jnp.concatenate([next_z[:, :, 512:], outer_half[:, :, :512]], 2),
            next_z,
            jnp.concatenate([far_z, next_z[:, :, :1024]], 2),
        ],
        z,
    )

    shares = mid_lift_product(mid_w, outer_one, mid_lift)
    every = over_leaf(gathered(over_sides(shares), 16)[1]).reshape(2, 8, 8, 768).transpose(1, 0, 2, 3)
    root_jump = over_blk(every)

    root_part = wide_product("root", root_jump, root_inverse)
    root_values, root_every = gathered(over_blk(root_part), 16)
    root_every = over_leaf(root_every)
    root_block = over_blk(root_every.reshape(8, 2, 8, 768))

    middle_part = wide_product("middle", root_block, mid_solve, mid_part)
    middle_values, middle_every = gathered(over_blk(middle_part), 8)
    middle_every = over_half(middle_every)

    root_half = lax.dynamic_slice_in_dim(root_every.reshape(2, 8, 8, 768), xl, 1, 0)[0]
    bound = jnp.concatenate(
        [
            root_half.transpose(1, 0, 2).reshape(8, 6144),
            middle_every.transpose(1, 0, 2).reshape(8, 4096),
        ],
        1,
    )
    bound = over_blk(bound.reshape(8, 8, 1280).transpose(1, 0, 2))
    lower_values = total(list(over_blk(last_product(bound, low_solve, low_part))))
    return (root_values, middle_values, lower_values)


def solution(mesh):
    placed = (P("blk", "leaf"),) + (P("leaf", "blk"),) * 7
    return jax.shard_map(
        local,
        mesh=mesh,
        in_specs=placed,
        out_specs=(P("blk", "leaf"),) * 3,
        check_vma=False,
    )
```

```python
import jax
import jax.numpy as jnp
from jax import lax
from jax.experimental import pallas as pl
from jax.experimental.pallas import tpu as pltpu
from jax.sharding import PartitionSpec as P

AXES = ("leaf", "blk")
DEVICES = [(s // 32, s // 8 % 4, s // 2 % 4, s % 2) for s in range(128)]
ROWS = (((1,), (1,)), ((), ()))


def flat(x, z, y, c):
    return ((x * 4 + z) * 4 + y) * 2 + c


def send(value, hop):
    pairs = []
    for source, place in enumerate(DEVICES):
        target = hop(*place)
        if target is not None:
            pairs.append((source, flat(*target)))
    return lax.ppermute(value, AXES, pairs)


def exchange(value, key, order):
    groups = {}
    for source, place in enumerate(DEVICES):
        groups.setdefault(key(*place), []).append((order(*place), source))
    members = [[source for _, source in sorted(group)] for group in groups.values()]
    return lax.all_to_all(value, AXES, 0, 0, axis_index_groups=members)


def over_blk(value):
    return exchange(value, lambda x, z, y, c: (x, z), lambda x, z, y, c: 2 * y + c)


def over_leaf(value):
    return exchange(value, lambda x, z, y, c: (y, c), lambda x, z, y, c: 4 * x + z)


def over_half(value):
    return exchange(value, lambda x, z, y, c: (x // 2, y, c), lambda x, z, y, c: 4 * x + z)


def over_z(value):
    return exchange(value, lambda x, z, y, c: (x, y, c), lambda x, z, y, c: z)


def over_y(value):
    return exchange(value, lambda x, z, y, c: (x, z, c), lambda x, z, y, c: y)


def over_zy(value):
    return exchange(value, lambda x, z, y, c: (x, c), lambda x, z, y, c: 4 * z + y)


def over_all(value):
    return exchange(value, lambda x, z, y, c: 0, flat)


def copies(value, number):
    return jnp.broadcast_to(value[None], (number, *value.shape))


def swap_core(value):
    return send(value, lambda x, z, y, c: (x, z, y, 1 - c))


def sum_y(value):
    return value + total([send(value, lambda x, z, y, c: (x, z, y ^ k, c)) for k in (1, 2, 3)])


def cols(value, start, size):
    return lax.dynamic_slice_in_dim(value, start, size, value.ndim - 1)


def pick(pieces, index):
    out = pieces[0]
    for number in range(1, len(pieces)):
        out = jnp.where(index == number, pieces[number], out)
    return out


def total(parts):
    out = parts[0]
    for part in parts[1:]:
        out = out + part
    return out


def place():
    leaf, blk = lax.axis_index("leaf"), lax.axis_index("blk")
    return leaf // 4, leaf % 4, blk // 2, blk % 2


def halves(value):
    high = value.astype(jnp.bfloat16)
    return high, (value - high.astype(jnp.float32)).astype(jnp.bfloat16)


def product(name, vectors, operator, inputs, outputs, store, tile, fetch=0):
    height, depth = operator.shape
    count, steps = len(inputs), height // tile

    def body(*refs):
        given, held, results = refs[:count], refs[count], refs[count + 1 :]
        moves = []
        if fetch:
            *results, room, sems = results
            for number in range(steps):
                here = pl.ds(number * tile, tile)
                moves.append(pltpu.make_async_copy(held.at[here], room.at[here], sems.at[number]))
                moves[-1].start()
            held = room
        high, low = halves(vectors(*given))
        both = jnp.concatenate([high, low], 0)
        for number in range(steps):
            if fetch:
                moves[number].wait()
            over, under = halves(held[number * tile : (number + 1) * tile, :])
            first = lax.dot_general(both, over, ROWS, preferred_element_type=jnp.float32)
            second = lax.dot_general(high, under, ROWS, preferred_element_type=jnp.float32)
            store(number, first[:64] + (first[64:] + second), *given, *results)

    block = pl.BlockSpec(memory_space=pltpu.VMEM)
    return pl.pallas_call(
        body,
        name=name,
        out_shape=[jax.ShapeDtypeStruct(shape, jnp.float32) for shape in outputs],
        in_specs=[block] * count + [pl.BlockSpec(memory_space=pl.ANY) if fetch else block],
        out_specs=[block] * len(outputs),
        scratch_shapes=[
            pltpu.VMEM((height, depth), jnp.float32),
            pltpu.SemaphoreType.DMA((steps,)),
        ]
        if fetch
        else [],
        compiler_params=pltpu.CompilerParams(vmem_limit_bytes=(fetch or 4) << 20),
        cost_estimate=pl.CostEstimate(
            flops=6 * 64 * height * depth, bytes_accessed=4 * height * depth, transcendentals=0
        ),
    )(*inputs, operator)


def gathered(parts, number):
    def body(parts, value, every):
        summed = total([parts[k] for k in range(parts.shape[0])])
        value[...] = summed
        for k in range(number):
            every[k] = summed

    shape = parts.shape[1:]
    return pl.pallas_call(
        body,
        name="gathered",
        out_shape=[
            jax.ShapeDtypeStruct(shape, jnp.float32),
            jax.ShapeDtypeStruct((number, *shape), jnp.float32),
        ],
        in_specs=[pl.BlockSpec(memory_space=pltpu.VMEM)],
        out_specs=[pl.BlockSpec(memory_space=pltpu.VMEM)] * 2,
        compiler_params=pltpu.CompilerParams(vmem_limit_bytes=4 << 20),
    )(parts)


def added(first, second, number=None):
    def body(first, second, out):
        if number is None:
            out[...] = first[...] + second[...]
        else:
            summed = first[...] + second[...]
            for k in range(number):
                out[k] = summed

    shape = first.shape if number is None else (number, *first.shape)
    return pl.pallas_call(
        body,
        name="added",
        out_shape=jax.ShapeDtypeStruct(shape, jnp.float32),
        in_specs=[pl.BlockSpec(memory_space=pltpu.VMEM)] * 2,
        out_specs=pl.BlockSpec(memory_space=pltpu.VMEM),
        compiler_params=pltpu.CompilerParams(vmem_limit_bytes=4 << 20),
    )(first, second)


def low_product(jump, operator):
    def vectors(jump):
        return (jump[12:16] - jump[4:8]).reshape(64, 512)

    def store(number, tile, jump, part, keep, give):
        part[:, 512 * number : 512 * (number + 1)] = tile
        core = place()[3]

        @pl.when(core == number)
        def _():
            keep[...] = tile

        @pl.when(core != number)
        def _():
            give[...] = tile

    shapes = [(64, 1024), (64, 512), (64, 512)]
    return product("low_w", vectors, operator, [jump], shapes, store, 512)


def lift_product(parts, particular, operator):
    def vectors(parts, particular):
        return parts[0] + parts[1] + (parts[2] + parts[3])

    def store(number, tile, parts, particular, keep, give, mine, other):
        x, z, y, c = place()
        if number == 0:
            keep[...] = jnp.zeros(keep.shape, jnp.float32)
            give[...] = jnp.zeros(give.shape, jnp.float32)
            for block in range(8):
                v, core = block // 2, block % 2
                source = 1024 + 512 * block if block < 7 else 0

                @pl.when((z == (2 if block < 7 else 3)) & (c == core))
                def _():
                    keep[y, v, pl.ds(pl.multiple_of(8 * c, 8), 8)] = particular[:, source : source + 512]

                @pl.when((z == (2 if block < 7 else 3)) & (c != core))
                def _():
                    give[y, v, pl.ds(pl.multiple_of(8 * c, 8), 8)] = particular[:, source : source + 512]

        here = pl.ds(512 * number, 512)
        block = number + jnp.where(z == 3, 3, -2)
        valid = (z == 3) | ((z == 2) & (number >= 2))
        row = jnp.clip(block // 2, 0, 3)

        @pl.when(valid & (block % 2 == c))
        def _():
            for k in range(4):
                keep[k, row] += tile[16 * k : 16 * k + 16]

        @pl.when(valid & (block % 2 != c))
        def _():
            for k in range(4):
                give[k, row] += tile[16 * k : 16 * k + 16]

        pairs = tile.reshape(4, 2, 8, 512)

        @pl.when(c == 0)
        def _():
            mine[:, :, here] = pairs[:, 0]
            other[:, :, here] = pairs[:, 1]

        @pl.when(c == 1)
        def _():
            mine[:, :, here] = pairs[:, 1]
            other[:, :, here] = pairs[:, 0]

    shapes = [(4, 4, 16, 512)] * 2 + [(4, 8, 2560)] * 2
    return product(
        "low_lift", vectors, operator, [parts, particular], shapes, store, 512
    )


def mid_product(parts, operator):
    def vectors(parts):
        return (parts[4:8] - parts[0:4]).reshape(64, 512)

    def store(number, tile, parts, out):
        out[:, 256 * number : 256 * (number + 1)] = tile

    return product("mid_w", vectors, operator, [parts], [(64, 512)], store, 256)[0]


def mid_lift_product(mid_w, outer, operator):
    def vectors(mid_w, outer):
        return mid_w[...]

    def store(number, tile, mid_w, outer, out):
        x, z, y, c = place()
        if number == 0:
            out[96:] = jnp.zeros((32, 8, 128), jnp.float32)
        added = outer[:, :, 256 * number : 256 * (number + 1)]
        sign = jnp.where(x // 2 == 1, 1.0, -1.0)
        pairs = tile.reshape(4, 2, 8, 256)
        for core in range(2):
            whole = sign * (pairs[:, core] + jnp.where(c == core, added, 0.0))
            for v in range(4):
                first = 12 * (2 * v + core) + 2 * number
                out[first] = whole[v, :, :128]
                out[first + 1] = whole[v, :, 128:]

    return product(
        "mid_lift", vectors, operator, [mid_w, outer], [(128, 8, 128)], store, 256
    )[0]


def mixed(parts):
    def body(parts, out):
        for block in range(8):
            given = [parts[64 * side + 8 * block + k] for side in range(2) for k in range(8)]
            summed = total(given)
            for leaf in range(16):
                out[8 * leaf + block] = summed

    return pl.pallas_call(
        body,
        name="mixed",
        out_shape=jax.ShapeDtypeStruct((128, 8, 128), jnp.float32),
        in_specs=[pl.BlockSpec(memory_space=pltpu.VMEM)],
        out_specs=pl.BlockSpec(memory_space=pltpu.VMEM),
        compiler_params=pltpu.CompilerParams(vmem_limit_bytes=4 << 20),
    )(parts)


def wide_product(name, parts, operator, added=None):
    height = operator.shape[0]

    def vectors(parts, *added):
        if parts.shape[0] == 128:
            lines = [
                jnp.concatenate([parts[12 * k + n] for n in range(12)], 1) for k in range(8)
            ]
            return jnp.concatenate(lines, 0)
        return jnp.concatenate([parts[:, 0].reshape(64, 768), parts[:, 1].reshape(64, 768)], 1)

    def store(number, tile, *refs):
        here = slice(256 * number, 256 * (number + 1))
        if len(refs) == 3:
            tile = tile + refs[1][:, here]
        refs[-1][:, :, here] = tile.reshape(8, 8, 256)

    inputs = [parts] if added is None else [parts, added]
    return product(name, vectors, operator, inputs, [(8, 8, height)], store, 256)[0]


def split_ahead(operator):
    def body(held, over, under):
        for number in range(4):
            here = slice(256 * number, 256 * (number + 1))
            over[here, :], under[here, :] = halves(held[here, :])

    return pl.pallas_call(
        body,
        name="split_ahead",
        out_shape=[jax.ShapeDtypeStruct(operator.shape, jnp.bfloat16)] * 2,
        in_specs=[pl.BlockSpec(memory_space=pltpu.VMEM)],
        out_specs=[pl.BlockSpec(memory_space=pltpu.VMEM)] * 2,
        compiler_params=pltpu.CompilerParams(vmem_limit_bytes=4 << 20),
    )(operator)


def last_product(bound, over, under, added):
    def body(bound, added, over, under, out):
        high, low = halves(bound[...].reshape(64, 1280))
        both = jnp.concatenate([high, low], 0)
        for number in range(4):
            here = slice(256 * number, 256 * (number + 1))
            first = lax.dot_general(both, over[here, :], ROWS, preferred_element_type=jnp.float32)
            second = lax.dot_general(high, under[here, :], ROWS, preferred_element_type=jnp.float32)
            tile = first[:64] + (first[64:] + second) + added[:, here]
            out[:, :, here] = tile.reshape(8, 8, 256)

    return pl.pallas_call(
        body,
        name="low_solve",
        out_shape=jax.ShapeDtypeStruct((8, 8, 1024), jnp.float32),
        in_specs=[pl.BlockSpec(memory_space=pltpu.VMEM)] * 4,
        out_specs=pl.BlockSpec(memory_space=pltpu.VMEM),
        compiler_params=pltpu.CompilerParams(vmem_limit_bytes=4 << 20),
    )(bound, added, over, under)


def local(
    particular, root_inverse, mid_inverse, low_inverse, mid_lift, low_lift, mid_solve, low_solve
):
    x, z, y, c = place()
    xh, xl = x // 2, x % 2

    inner = particular[:, 512:].reshape(8, 4, 2, 512)
    keep = lax.dynamic_index_in_dim(inner, c, 2, False).transpose(1, 0, 2)
    got = swap_core(lax.dynamic_index_in_dim(inner, 1 - c, 2, False).transpose(1, 0, 2))
    both = jnp.concatenate([jnp.where(c == 0, keep, got), jnp.where(c == 0, got, keep)], 1)
    jump_two = over_zy(copies(both, 4).reshape(16, 16, 512))

    low_part, keep, give = low_product(jump_two, low_inverse)
    low_w = over_y(over_z(added(keep, swap_core(give), 4)))

    keep, give, mine, other = lift_product(low_w, particular, low_lift)

    blocks = added(keep, swap_core(give)).reshape(16, 16, 512)
    blocks, other, apart = lax.optimization_barrier((blocks, other, particular))
    jump_one = over_half(gathered(over_zy(blocks), 8)[1])

    mid_part = mid_product(jump_one, mid_inverse)
    mid_sum = sum_y(mid_part + swap_core(mid_part))
    mid_w = send(
        mid_sum, lambda x, z, y, c: (x // 2 * 2 + c, y ^ z, x % 2 * 2 + z // 2, z % 2)
    )

    here = (jnp.arange(4) == y)[:, None, None]
    nothing = jnp.zeros((8, 2048), jnp.float32)
    outer = jnp.where(
        z == 1, jnp.concatenate([nothing, apart[:, :512]], 1), apart[:, :2560]
    )
    outer_half = mine + swap_core(other) + jnp.where(here, outer[None], 0.0)
    beyond = jnp.where(here, apart[None, :, 2560:3072], 0.0)
    next_z = send(
        pick(
            [
                jnp.concatenate([beyond, outer_half[:, :, 1536:]], 2),
                outer_half[:, :, 512:2048],
                outer_half[:, :, :1536],
            ],
            z,
        ),
        lambda x, z, y, c: (x, z + 1, y, c) if z < 3 else None,
    )
    thirds = apart[:, 3072:].reshape(8, 3, 512).transpose(1, 0, 2)
    far_z = send(
        jnp.where(
            z == 0,
            jnp.concatenate([thirds, jnp.zeros((1, 8, 512), jnp.float32)], 0),
            outer_half[:, :, 2048:],
        ),
        lambda x, z, y, c: (x, z + 2, y, c) if z < 2 else None,
    )
    wide = jnp.concatenate([far_z[0], far_z[1], far_z[2]], 1)
    outer_one = pick(
        [
            outer_half[:, :, :1536],
            jnp.concatenate([next_z[:, :, 512:], outer_half[:, :, :512] + next_z[:, :, :512]], 2),
            next_z + jnp.where(here, wide[None], 0.0),
            jnp.concatenate([far_z, next_z[:, :, :1024]], 2),
        ],
        z,
    )

    shares = mid_lift_product(mid_w, outer_one, mid_lift)
    root_jump = over_all(mixed(over_all(shares)))

    root_part = wide_product("root", root_jump, root_inverse)
    root_values, root_every = gathered(over_blk(root_part), 16)
    root_every = over_leaf(root_every)
    root_block = over_blk(root_every.reshape(8, 2, 8, 768))

    middle_part = wide_product("middle", root_block, mid_solve, mid_part)
    middle_values, middle_every = gathered(over_blk(middle_part), 8)
    middle_every, low_solve = lax.optimization_barrier((middle_every, low_solve))
    middle_every = over_half(middle_every)
    over, under = split_ahead(low_solve)

    root_half = lax.dynamic_slice_in_dim(root_every.reshape(2, 8, 8, 768), xl, 1, 0)[0]
    bound = jnp.concatenate(
        [
            root_half.transpose(1, 0, 2).reshape(8, 6144),
            middle_every.transpose(1, 0, 2).reshape(8, 4096),
        ],
        1,
    )
    bound = over_blk(bound.reshape(8, 8, 1280).transpose(1, 0, 2))
    lower_values = total(list(over_blk(last_product(bound, over, under, low_part))))
    return (root_values, middle_values, lower_values)


def solution(mesh):
    placed = (P("blk", "leaf"),) + (P("leaf", "blk"),) * 7
    return jax.shard_map(
        local,
        mesh=mesh,
        in_specs=placed,
        out_specs=(P("blk", "leaf"),) * 3,
        check_vma=False,
    )
```

```python
import jax
import jax.numpy as jnp
from jax import lax
from jax.experimental import pallas as pl
from jax.experimental.pallas import tpu as pltpu
from jax.sharding import PartitionSpec as P

AXES = ("leaf", "blk")
DEVICES = [(s // 32, s // 8 % 4, s // 2 % 4, s % 2) for s in range(128)]
ROWS = (((1,), (1,)), ((), ()))


def flat(x, z, y, c):
    return ((x * 4 + z) * 4 + y) * 2 + c


def send(value, hop):
    pairs = []
    for source, place in enumerate(DEVICES):
        target = hop(*place)
        if target is not None:
            pairs.append((source, flat(*target)))
    return lax.ppermute(value, AXES, pairs)


def exchange(value, key, order):
    groups = {}
    for source, place in enumerate(DEVICES):
        groups.setdefault(key(*place), []).append((order(*place), source))
    members = [[source for _, source in sorted(group)] for group in groups.values()]
    return lax.all_to_all(value, AXES, 0, 0, axis_index_groups=members)


def over_blk(value):
    return exchange(value, lambda x, z, y, c: (x, z), lambda x, z, y, c: 2 * y + c)


def over_leaf(value):
    return exchange(value, lambda x, z, y, c: (y, c), lambda x, z, y, c: 4 * x + z)


def over_half(value):
    return exchange(value, lambda x, z, y, c: (x // 2, y, c), lambda x, z, y, c: 4 * x + z)


def over_low(value):
    return exchange(value, lambda x, z, y, c: (x // 2, c), lambda x, z, y, c: (x, z, y))


def over_zy(value):
    return exchange(value, lambda x, z, y, c: (x, c), lambda x, z, y, c: 4 * z + y)


def over_all(value):
    return exchange(value, lambda x, z, y, c: 0, flat)


def copies(value, number):
    return jnp.broadcast_to(value[None], (number, *value.shape))


def swap_core(value):
    return send(value, lambda x, z, y, c: (x, z, y, 1 - c))


def sum_y(value):
    return value + total([send(value, lambda x, z, y, c: (x, z, y ^ k, c)) for k in (1, 2, 3)])


def cols(value, start, size):
    return lax.dynamic_slice_in_dim(value, start, size, value.ndim - 1)


def pick(pieces, index):
    out = pieces[0]
    for number in range(1, len(pieces)):
        out = jnp.where(index == number, pieces[number], out)
    return out


def total(parts):
    out = parts[0]
    for part in parts[1:]:
        out = out + part
    return out


def place():
    leaf, blk = lax.axis_index("leaf"), lax.axis_index("blk")
    return leaf // 4, leaf % 4, blk // 2, blk % 2


def halves(value):
    high = value.astype(jnp.bfloat16)
    return high, (value - high.astype(jnp.float32)).astype(jnp.bfloat16)


def product(name, vectors, operator, inputs, outputs, store, tile, fetch=0):
    height, depth = operator.shape
    count, steps = len(inputs), height // tile

    def body(*refs):
        given, held, results = refs[:count], refs[count], refs[count + 1 :]
        moves = []
        if fetch:
            *results, room, sems = results
            for number in range(steps):
                here = pl.ds(number * tile, tile)
                moves.append(pltpu.make_async_copy(held.at[here], room.at[here], sems.at[number]))
                moves[-1].start()
            held = room
        high, low = halves(vectors(*given))
        both = jnp.concatenate([high, low], 0)
        for number in range(steps):
            if fetch:
                moves[number].wait()
            over, under = halves(held[number * tile : (number + 1) * tile, :])
            first = lax.dot_general(both, over, ROWS, preferred_element_type=jnp.float32)
            second = lax.dot_general(high, under, ROWS, preferred_element_type=jnp.float32)
            store(number, first[:64] + (first[64:] + second), *given, *results)

    block = pl.BlockSpec(memory_space=pltpu.VMEM)
    return pl.pallas_call(
        body,
        name=name,
        out_shape=[jax.ShapeDtypeStruct(shape, jnp.float32) for shape in outputs],
        in_specs=[block] * count + [pl.BlockSpec(memory_space=pl.ANY) if fetch else block],
        out_specs=[block] * len(outputs),
        scratch_shapes=[
            pltpu.VMEM((height, depth), jnp.float32),
            pltpu.SemaphoreType.DMA((steps,)),
        ]
        if fetch
        else [],
        compiler_params=pltpu.CompilerParams(vmem_limit_bytes=(fetch or 4) << 20),
        cost_estimate=pl.CostEstimate(
            flops=6 * 64 * height * depth, bytes_accessed=4 * height * depth, transcendentals=0
        ),
    )(*inputs, operator)


def gathered(parts, number):
    parts = parts if isinstance(parts, list) else [parts]
    count = len(parts)

    def body(*refs):
        value, every = refs[count:]
        if count == 1:
            summed = total([refs[0][k] for k in range(refs[0].shape[0])])
        else:
            summed = total([ref[...] for ref in refs[:count]])
        value[...] = summed
        for k in range(number):
            every[k] = summed

    shape = parts[0].shape[1:] if count == 1 else parts[0].shape
    block = pl.BlockSpec(memory_space=pltpu.VMEM)
    return pl.pallas_call(
        body,
        name="gathered",
        out_shape=[
            jax.ShapeDtypeStruct(shape, jnp.float32),
            jax.ShapeDtypeStruct((number, *shape), jnp.float32),
        ],
        in_specs=[block] * count,
        out_specs=[block] * 2,
        compiler_params=pltpu.CompilerParams(vmem_limit_bytes=4 << 20),
    )(*parts)


def added(first, second, number=None):
    def body(first, second, out):
        if number is None:
            out[...] = first[...] + second[...]
        else:
            summed = first[...] + second[...]
            for k in range(number):
                out[k] = summed

    shape = first.shape if number is None else (number, *first.shape)
    return pl.pallas_call(
        body,
        name="added",
        out_shape=jax.ShapeDtypeStruct(shape, jnp.float32),
        in_specs=[pl.BlockSpec(memory_space=pltpu.VMEM)] * 2,
        out_specs=pl.BlockSpec(memory_space=pltpu.VMEM),
        compiler_params=pltpu.CompilerParams(vmem_limit_bytes=4 << 20),
    )(first, second)


def low_product(jump, operator):
    def vectors(jump):
        return (jump[12:16] - jump[4:8]).reshape(64, 512)

    def store(number, tile, jump, part, keep, give):
        part[:, 512 * number : 512 * (number + 1)] = tile
        mine = place()[3] == number
        keep[...] = jnp.where(mine, tile, keep[...])
        give[...] = jnp.where(mine, give[...], tile)

    shapes = [(64, 1024), (64, 512), (64, 512)]
    return product("low_w", vectors, operator, [jump], shapes, store, 512)


def turned(parts):
    def body(*refs):
        x, z, y, c = place()
        for shift in range(4):

            @pl.when(z ^ y == shift)
            def _():
                for k in range(4):
                    refs[4 + k][...] = refs[shift ^ k][...]

    block = pl.BlockSpec(memory_space=pltpu.VMEM)
    return pl.pallas_call(
        body,
        name="turned",
        out_shape=[jax.ShapeDtypeStruct(parts[0].shape, jnp.float32)] * 4,
        in_specs=[block] * 4,
        out_specs=[block] * 4,
        compiler_params=pltpu.CompilerParams(vmem_limit_bytes=4 << 20),
    )(*parts)


def lift_product(parts, particular, operator):
    def vectors(*refs):
        return refs[0][...] + refs[1][...] + (refs[2][...] + refs[3][...])

    def store(number, tile, *refs):
        particular, keep, give, mine, other = refs[4:]
        x, z, y, c = place()
        sign = jnp.where(x % 2 == 1, 1.0, -1.0)
        if number == 0:
            keep[...] = jnp.zeros(keep.shape, jnp.float32)
            give[...] = jnp.zeros(give.shape, jnp.float32)
            for block in range(8):
                v, core = block // 2, block % 2
                source = 1024 + 512 * block if block < 7 else 0

                @pl.when((z == (2 if block < 7 else 3)) & (c == core))
                def _():
                    keep[2 * y + c, v] = sign * particular[:, source : source + 512]

                @pl.when((z == (2 if block < 7 else 3)) & (c != core))
                def _():
                    give[2 * y + c, v] = sign * particular[:, source : source + 512]

        here = pl.ds(512 * number, 512)
        block = number + jnp.where(z == 3, 3, -2)
        valid = (z == 3) | ((z == 2) & (number >= 2))
        row = jnp.clip(block // 2, 0, 3)

        @pl.when(valid & (block % 2 == c))
        def _():
            for k in range(8):
                keep[k, row] += sign * tile[8 * k : 8 * k + 8]

        @pl.when(valid & (block % 2 != c))
        def _():
            for k in range(8):
                give[k, row] += sign * tile[8 * k : 8 * k + 8]

        shared(tile, here, mine, other)

    shapes = [(8, 4, 8, 512)] * 2 + [(4, 8, 2560)] * 2
    return product(
        "low_lift", vectors, operator, [*parts, particular], shapes, store, 512
    )


def mid_product(parts, operator):
    def vectors(parts):
        return parts[...].reshape(64, 512)

    def store(number, tile, parts, out):
        out[:, 256 * number : 256 * (number + 1)] = tile

    return product("mid_w", vectors, operator, [parts], [(64, 512)], store, 256)[0]


def mid_lift_product(mid_w, outer, operator):
    def vectors(mid_w, outer):
        return mid_w[...]

    def store(number, tile, mid_w, outer, out):
        x, z, y, c = place()
        if number == 0:
            out[96:] = jnp.zeros((32, 8, 128), jnp.float32)
        added = outer[:, :, 256 * number : 256 * (number + 1)]
        sign = jnp.where(x // 2 == 1, 1.0, -1.0)
        pairs = tile.reshape(4, 2, 8, 256)
        for core in range(2):
            whole = sign * (pairs[:, core] + jnp.where(c == core, added, 0.0))
            for v in range(4):
                first = 12 * (2 * v + core) + 2 * number
                out[first] = whole[v, :, :128]
                out[first + 1] = whole[v, :, 128:]

    return product(
        "mid_lift", vectors, operator, [mid_w, outer], [(128, 8, 128)], store, 256
    )[0]


def mixed(parts):
    def body(parts, out):
        for block in range(8):
            given = [parts[64 * side + 8 * block + k] for side in range(2) for k in range(8)]
            summed = total(given)
            for leaf in range(16):
                out[8 * leaf + block] = summed

    return pl.pallas_call(
        body,
        name="mixed",
        out_shape=jax.ShapeDtypeStruct((128, 8, 128), jnp.float32),
        in_specs=[pl.BlockSpec(memory_space=pltpu.VMEM)],
        out_specs=pl.BlockSpec(memory_space=pltpu.VMEM),
        compiler_params=pltpu.CompilerParams(vmem_limit_bytes=4 << 20),
    )(parts)


def shared(tile, here, keep, give):
    first = place()[3] == 0
    pairs = tile.reshape(4, 2, 8, tile.shape[1])
    keep[:, :, here] = jnp.where(first, pairs[:, 0], pairs[:, 1])
    give[:, :, here] = jnp.where(first, pairs[:, 1], pairs[:, 0])


def over_columns(keep, give):
    def body(keep, got, *out):
        y = place()[2]
        for mine in range(4):

            @pl.when(y == mine)
            def _():
                for k in range(4):
                    out[k][...] = keep[mine ^ k] + got[mine ^ k]

    block = pl.BlockSpec(memory_space=pltpu.VMEM)
    parts = pl.pallas_call(
        body,
        name="over_columns",
        out_shape=[jax.ShapeDtypeStruct(keep.shape[1:], jnp.float32)] * 4,
        in_specs=[block] * 2,
        out_specs=[block] * 4,
        compiler_params=pltpu.CompilerParams(vmem_limit_bytes=4 << 20),
    )(keep, swap_core(give))
    return [parts[0]] + [
        send(parts[k], lambda x, z, y, c: (x, z, y ^ k, c)) for k in (1, 2, 3)
    ]


def wide_product(name, parts, operator, added=None):
    height = operator.shape[0]

    def vectors(parts, *added):
        if parts.shape[0] == 128:
            lines = [
                jnp.concatenate([parts[12 * k + n] for n in range(12)], 1) for k in range(8)
            ]
            return jnp.concatenate(lines, 0)
        return jnp.concatenate([parts[:, 0].reshape(64, 768), parts[:, 1].reshape(64, 768)], 1)

    def store(number, tile, *refs):
        here = slice(256 * number, 256 * (number + 1))
        if len(refs) == 4:
            tile = tile + refs[1][:, here]
        shared(tile, here, *refs[-2:])

    inputs = [parts] if added is None else [parts, added]
    return product(name, vectors, operator, inputs, [(4, 8, height)] * 2, store, 256)


def split_ahead(operator):
    def body(held, over, under):
        for number in range(4):
            here = slice(256 * number, 256 * (number + 1))
            over[here, :], under[here, :] = halves(held[here, :])

    return pl.pallas_call(
        body,
        name="split_ahead",
        out_shape=[jax.ShapeDtypeStruct(operator.shape, jnp.bfloat16)] * 2,
        in_specs=[pl.BlockSpec(memory_space=pltpu.VMEM)],
        out_specs=[pl.BlockSpec(memory_space=pltpu.VMEM)] * 2,
        compiler_params=pltpu.CompilerParams(vmem_limit_bytes=4 << 20),
    )(operator)


def last_product(bound, over, under, added):
    def body(bound, added, over, under, keep, give):
        high, low = halves(bound[...].reshape(64, 1280))
        both = jnp.concatenate([high, low], 0)
        for number in range(4):
            here = slice(256 * number, 256 * (number + 1))
            first = lax.dot_general(both, over[here, :], ROWS, preferred_element_type=jnp.float32)
            second = lax.dot_general(high, under[here, :], ROWS, preferred_element_type=jnp.float32)
            tile = first[:64] + (first[64:] + second) + added[:, here]
            shared(tile, here, keep, give)

    return pl.pallas_call(
        body,
        name="low_solve",
        out_shape=[jax.ShapeDtypeStruct((4, 8, 1024), jnp.float32)] * 2,
        in_specs=[pl.BlockSpec(memory_space=pltpu.VMEM)] * 4,
        out_specs=[pl.BlockSpec(memory_space=pltpu.VMEM)] * 2,
        compiler_params=pltpu.CompilerParams(vmem_limit_bytes=4 << 20),
    )(bound, added, over, under)


def local(
    particular, root_inverse, mid_inverse, low_inverse, mid_lift, low_lift, mid_solve, low_solve
):
    x, z, y, c = place()
    xh, xl = x // 2, x % 2

    inner = particular[:, 512:].reshape(8, 4, 2, 512)
    keep = lax.dynamic_index_in_dim(inner, c, 2, False).transpose(1, 0, 2)
    got = swap_core(lax.dynamic_index_in_dim(inner, 1 - c, 2, False).transpose(1, 0, 2))
    both = jnp.concatenate([jnp.where(c == 0, keep, got), jnp.where(c == 0, got, keep)], 1)
    jump_two = over_zy(copies(both, 4).reshape(16, 16, 512))

    low_part, keep, give = low_product(jump_two, low_inverse)
    half = added(keep, swap_core(give))
    blocks = [half] + [send(half, lambda x, z, y, c: (x, z ^ k, y, c)) for k in (1, 2, 3)]
    blocks = list(turned(blocks))
    low_w = blocks[:1] + [
        send(blocks[k], lambda x, z, y, c: (x, z, y ^ k, c)) for k in (1, 2, 3)
    ]

    keep, give, mine, other = lift_product(low_w, particular, low_lift)

    blocks = added(keep, swap_core(give)).reshape(32, 8, 512)
    blocks, other, apart = lax.optimization_barrier((blocks, other, particular))
    jump_one = over_half(gathered(over_low(blocks), 8)[1])

    mid_part = mid_product(jump_one, mid_inverse)
    mid_sum = sum_y(mid_part + swap_core(mid_part))
    mid_w = send(
        mid_sum, lambda x, z, y, c: (x // 2 * 2 + c, y ^ z, x % 2 * 2 + z // 2, z % 2)
    )

    here = (jnp.arange(4) == y)[:, None, None]
    nothing = jnp.zeros((8, 2048), jnp.float32)
    outer = jnp.where(
        z == 1, jnp.concatenate([nothing, apart[:, :512]], 1), apart[:, :2560]
    )
    outer_half = mine + swap_core(other) + jnp.where(here, outer[None], 0.0)
    beyond = jnp.where(here, apart[None, :, 2560:3072], 0.0)
    next_z = send(
        pick(
            [
                jnp.concatenate([beyond, outer_half[:, :, 1536:]], 2),
                outer_half[:, :, 512:2048],
                outer_half[:, :, :1536],
            ],
            z,
        ),
        lambda x, z, y, c: (x, z + 1, y, c) if z < 3 else None,
    )
    thirds = apart[:, 3072:].reshape(8, 3, 512).transpose(1, 0, 2)
    far_z = send(
        jnp.where(
            z == 0,
            jnp.concatenate([thirds, jnp.zeros((1, 8, 512), jnp.float32)], 0),
            outer_half[:, :, 2048:],
        ),
        lambda x, z, y, c: (x, z + 2, y, c) if z < 2 else None,
    )
    wide = jnp.concatenate([far_z[0], far_z[1], far_z[2]], 1)
    outer_one = pick(
        [
            outer_half[:, :, :1536],
            jnp.concatenate([next_z[:, :, 512:], outer_half[:, :, :512] + next_z[:, :, :512]], 2),
            next_z + jnp.where(here, wide[None], 0.0),
            jnp.concatenate([far_z, next_z[:, :, :1024]], 2),
        ],
        z,
    )

    shares = mid_lift_product(mid_w, outer_one, mid_lift)
    root_jump = over_all(mixed(over_all(shares)))

    root_part = wide_product("root", root_jump, root_inverse)
    root_values, root_every = gathered(over_columns(*root_part), 16)
    root_every = over_leaf(root_every)
    root_block = over_blk(root_every.reshape(8, 2, 8, 768))

    middle_part = wide_product("middle", root_block, mid_solve, mid_part)
    middle_values, middle_every = gathered(over_columns(*middle_part), 8)
    middle_every, low_solve = lax.optimization_barrier((middle_every, low_solve))
    middle_every = over_half(middle_every)
    over, under = split_ahead(low_solve)

    root_half = lax.dynamic_slice_in_dim(root_every.reshape(2, 8, 8, 768), xl, 1, 0)[0]
    bound = jnp.concatenate(
        [
            root_half.transpose(1, 0, 2).reshape(8, 6144),
            middle_every.transpose(1, 0, 2).reshape(8, 4096),
        ],
        1,
    )
    bound = over_blk(bound.reshape(8, 8, 1280).transpose(1, 0, 2))
    lower_values = total(over_columns(*last_product(bound, over, under, low_part)))
    return (root_values, middle_values, lower_values)


def solution(mesh):
    placed = (P("blk", "leaf"),) + (P("leaf", "blk"),) * 7
    return jax.shard_map(
        local,
        mesh=mesh,
        in_specs=placed,
        out_specs=(P("blk", "leaf"),) * 3,
        check_vma=False,
    )
```

```python
import jax
import jax.numpy as jnp
from jax import lax
from jax.experimental import pallas as pl
from jax.experimental.pallas import tpu as pltpu
from jax.sharding import PartitionSpec as P

AXES = ("leaf", "blk")
DEVICES = [(s // 32, s // 8 % 4, s // 2 % 4, s % 2) for s in range(128)]
ROWS = (((1,), (1,)), ((), ()))


def flat(x, z, y, c):
    return ((x * 4 + z) * 4 + y) * 2 + c


def send(value, hop):
    pairs = []
    for source, place in enumerate(DEVICES):
        target = hop(*place)
        if target is not None:
            pairs.append((source, flat(*target)))
    return lax.ppermute(value, AXES, pairs)


def exchange(value, key, order):
    groups = {}
    for source, place in enumerate(DEVICES):
        groups.setdefault(key(*place), []).append((order(*place), source))
    members = [[source for _, source in sorted(group)] for group in groups.values()]
    return lax.all_to_all(value, AXES, 0, 0, axis_index_groups=members)


def over_blk(value):
    return exchange(value, lambda x, z, y, c: (x, z), lambda x, z, y, c: 2 * y + c)


def over_leaf(value):
    return exchange(value, lambda x, z, y, c: (y, c), lambda x, z, y, c: 4 * x + z)


def over_half(value):
    return exchange(value, lambda x, z, y, c: (x // 2, y, c), lambda x, z, y, c: 4 * x + z)


def over_low(value):
    return exchange(value, lambda x, z, y, c: (x // 2, c), lambda x, z, y, c: (x, z, y))


def over_zy(value):
    return exchange(value, lambda x, z, y, c: (x, c), lambda x, z, y, c: 4 * z + y)


def over_all(value):
    return exchange(value, lambda x, z, y, c: 0, flat)


def copies(value, number):
    return jnp.broadcast_to(value[None], (number, *value.shape))


def swap_core(value):
    return send(value, lambda x, z, y, c: (x, z, y, 1 - c))


def sum_y(value):
    return value + total([send(value, lambda x, z, y, c: (x, z, y ^ k, c)) for k in (1, 2, 3)])


def cols(value, start, size):
    return lax.dynamic_slice_in_dim(value, start, size, value.ndim - 1)


def pick(pieces, index):
    out = pieces[0]
    for number in range(1, len(pieces)):
        out = jnp.where(index == number, pieces[number], out)
    return out


def total(parts):
    out = parts[0]
    for part in parts[1:]:
        out = out + part
    return out


def place():
    leaf, blk = lax.axis_index("leaf"), lax.axis_index("blk")
    return leaf // 4, leaf % 4, blk // 2, blk % 2


def halves(value):
    high = value.astype(jnp.bfloat16)
    return high, (value - high.astype(jnp.float32)).astype(jnp.bfloat16)


def product(name, vectors, operator, inputs, outputs, store, tile, fetch=0):
    height, depth = operator.shape
    count, steps = len(inputs), height // tile

    def body(*refs):
        given, held, results = refs[:count], refs[count], refs[count + 1 :]
        moves = []
        if fetch:
            *results, room, sems = results
            for number in range(steps):
                here = pl.ds(number * tile, tile)
                moves.append(pltpu.make_async_copy(held.at[here], room.at[here], sems.at[number]))
                moves[-1].start()
            held = room
        high, low = halves(vectors(*given))
        both = jnp.concatenate([high, low], 0)
        for number in range(steps):
            if fetch:
                moves[number].wait()
            over, under = halves(held[number * tile : (number + 1) * tile, :])
            first = lax.dot_general(both, over, ROWS, preferred_element_type=jnp.float32)
            second = lax.dot_general(high, under, ROWS, preferred_element_type=jnp.float32)
            store(number, first[:64] + (first[64:] + second), *given, *results)

    block = pl.BlockSpec(memory_space=pltpu.VMEM)
    return pl.pallas_call(
        body,
        name=name,
        out_shape=[jax.ShapeDtypeStruct(shape, jnp.float32) for shape in outputs],
        in_specs=[block] * count + [pl.BlockSpec(memory_space=pl.ANY) if fetch else block],
        out_specs=[block] * len(outputs),
        scratch_shapes=[
            pltpu.VMEM((height, depth), jnp.float32),
            pltpu.SemaphoreType.DMA((steps,)),
        ]
        if fetch
        else [],
        compiler_params=pltpu.CompilerParams(vmem_limit_bytes=(fetch or 4) << 20),
        cost_estimate=pl.CostEstimate(
            flops=6 * 64 * height * depth, bytes_accessed=4 * height * depth, transcendentals=0
        ),
    )(*inputs, operator)


def gathered(parts, number):
    parts = parts if isinstance(parts, list) else [parts]
    count = len(parts)

    def body(*refs):
        value, every = refs[count:]
        if count == 1:
            summed = total([refs[0][k] for k in range(refs[0].shape[0])])
        else:
            summed = total([ref[...] for ref in refs[:count]])
        value[...] = summed
        for k in range(number):
            every[k] = summed

    shape = parts[0].shape[1:] if count == 1 else parts[0].shape
    block = pl.BlockSpec(memory_space=pltpu.VMEM)
    return pl.pallas_call(
        body,
        name="gathered",
        out_shape=[
            jax.ShapeDtypeStruct(shape, jnp.float32),
            jax.ShapeDtypeStruct((number, *shape), jnp.float32),
        ],
        in_specs=[block] * count,
        out_specs=[block] * 2,
        compiler_params=pltpu.CompilerParams(vmem_limit_bytes=4 << 20),
    )(*parts)


def added(first, second, number=None):
    def body(first, second, out):
        if number is None:
            out[...] = first[...] + second[...]
        else:
            summed = first[...] + second[...]
            for k in range(number):
                out[k] = summed

    shape = first.shape if number is None else (number, *first.shape)
    return pl.pallas_call(
        body,
        name="added",
        out_shape=jax.ShapeDtypeStruct(shape, jnp.float32),
        in_specs=[pl.BlockSpec(memory_space=pltpu.VMEM)] * 2,
        out_specs=pl.BlockSpec(memory_space=pltpu.VMEM),
        compiler_params=pltpu.CompilerParams(vmem_limit_bytes=4 << 20),
    )(first, second)


def low_product(jump, operator):
    def vectors(jump):
        return (jump[12:16] - jump[4:8]).reshape(64, 512)

    def store(number, tile, jump, part, keep, give):
        part[:, 512 * number : 512 * (number + 1)] = tile
        mine = place()[3] == number
        keep[...] = jnp.where(mine, tile, keep[...])
        give[...] = jnp.where(mine, give[...], tile)

    shapes = [(64, 1024), (64, 512), (64, 512)]
    return product("low_w", vectors, operator, [jump], shapes, store, 512)


def turned(parts):
    def body(*refs):
        x, z, y, c = place()
        for shift in range(4):

            @pl.when(z ^ y == shift)
            def _():
                for k in range(4):
                    refs[4 + k][...] = refs[shift ^ k][...]

    block = pl.BlockSpec(memory_space=pltpu.VMEM)
    return pl.pallas_call(
        body,
        name="turned",
        out_shape=[jax.ShapeDtypeStruct(parts[0].shape, jnp.float32)] * 4,
        in_specs=[block] * 4,
        out_specs=[block] * 4,
        compiler_params=pltpu.CompilerParams(vmem_limit_bytes=4 << 20),
    )(*parts)


def lift_product(parts, particular, operator):
    def vectors(*refs):
        return refs[0][...] + refs[1][...] + (refs[2][...] + refs[3][...])

    def store(number, tile, *refs):
        particular, keep, give, mine, other = refs[4:]
        x, z, y, c = place()
        sign = jnp.where(x % 2 == 1, 1.0, -1.0)
        if number == 0:
            keep[...] = jnp.zeros(keep.shape, jnp.float32)
            give[...] = jnp.zeros(give.shape, jnp.float32)
            for block in range(8):
                v, core = block // 2, block % 2
                source = 1024 + 512 * block if block < 7 else 0

                @pl.when((z == (2 if block < 7 else 3)) & (c == core))
                def _():
                    keep[2 * y + c, v] = sign * particular[:, source : source + 512]

                @pl.when((z == (2 if block < 7 else 3)) & (c != core))
                def _():
                    give[2 * y + c, v] = sign * particular[:, source : source + 512]

        here = pl.ds(512 * number, 512)
        block = number + jnp.where(z == 3, 3, -2)
        valid = (z == 3) | ((z == 2) & (number >= 2))
        row = jnp.clip(block // 2, 0, 3)

        @pl.when(valid & (block % 2 == c))
        def _():
            for k in range(8):
                keep[k, row] += sign * tile[8 * k : 8 * k + 8]

        @pl.when(valid & (block % 2 != c))
        def _():
            for k in range(8):
                give[k, row] += sign * tile[8 * k : 8 * k + 8]

        shared(tile, here, mine, other)

    shapes = [(8, 4, 8, 512)] * 2 + [(4, 8, 2560)] * 2
    return product(
        "low_lift", vectors, operator, [*parts, particular], shapes, store, 512
    )


def mid_product(parts, operator):
    def vectors(parts):
        return parts[...].reshape(64, 512)

    def store(number, tile, parts, out):
        out[:, 256 * number : 256 * (number + 1)] = tile

    return product("mid_w", vectors, operator, [parts], [(64, 512)], store, 256)[0]


def mid_lift_product(mid_w, outer, operator):
    def vectors(mid_w, outer):
        return mid_w[...]

    def store(number, tile, mid_w, outer, out):
        x, z, y, c = place()
        if number == 0:
            out[96:] = jnp.zeros((32, 8, 128), jnp.float32)
        added = outer[:, :, 256 * number : 256 * (number + 1)]
        sign = jnp.where(x // 2 == 1, 1.0, -1.0)
        pairs = tile.reshape(4, 2, 8, 256)
        for core in range(2):
            whole = sign * (pairs[:, core] + jnp.where(c == core, added, 0.0))
            for v in range(4):
                first = 12 * (2 * v + core) + 2 * number
                out[first] = whole[v, :, :128]
                out[first + 1] = whole[v, :, 128:]

    return product(
        "mid_lift", vectors, operator, [mid_w, outer], [(128, 8, 128)], store, 256
    )[0]


def mixed(parts):
    def body(parts, out):
        for block in range(8):
            given = [parts[64 * side + 8 * block + k] for side in range(2) for k in range(8)]
            summed = total(given)
            for leaf in range(16):
                out[8 * leaf + block] = summed

    return pl.pallas_call(
        body,
        name="mixed",
        out_shape=jax.ShapeDtypeStruct((128, 8, 128), jnp.float32),
        in_specs=[pl.BlockSpec(memory_space=pltpu.VMEM)],
        out_specs=pl.BlockSpec(memory_space=pltpu.VMEM),
        compiler_params=pltpu.CompilerParams(vmem_limit_bytes=4 << 20),
    )(parts)


def shared(tile, here, keep, give):
    first = place()[3] == 0
    pairs = tile.reshape(4, 2, 8, tile.shape[1])
    keep[:, :, here] = jnp.where(first, pairs[:, 0], pairs[:, 1])
    give[:, :, here] = jnp.where(first, pairs[:, 1], pairs[:, 0])


def over_columns(keep, give):
    def body(keep, got, *out):
        y = place()[2]
        for mine in range(4):

            @pl.when(y == mine)
            def _():
                for k in range(4):
                    out[k][...] = keep[mine ^ k] + got[mine ^ k]

    block = pl.BlockSpec(memory_space=pltpu.VMEM)
    parts = pl.pallas_call(
        body,
        name="over_columns",
        out_shape=[jax.ShapeDtypeStruct(keep.shape[1:], jnp.float32)] * 4,
        in_specs=[block] * 2,
        out_specs=[block] * 4,
        compiler_params=pltpu.CompilerParams(vmem_limit_bytes=4 << 20),
    )(keep, swap_core(give))
    return [parts[0]] + [
        send(parts[k], lambda x, z, y, c: (x, z, y ^ k, c)) for k in (1, 2, 3)
    ]


def to_columns(keep, give):
    def body(keep, got, *out):
        x, z, y, c = place()
        for mine in range(4):

            @pl.when(y == mine)
            def _():
                for k in range(4):
                    own, other = keep[mine ^ k], got[mine ^ k]
                    out[k][0:8] = jnp.where(c == 0, own, other)
                    out[k][8:16] = jnp.where(c == 0, other, own)

    block = pl.BlockSpec(memory_space=pltpu.VMEM)
    parts = pl.pallas_call(
        body,
        name="to_columns",
        out_shape=[jax.ShapeDtypeStruct((16, keep.shape[2]), jnp.float32)] * 4,
        in_specs=[block] * 2,
        out_specs=[block] * 4,
        compiler_params=pltpu.CompilerParams(vmem_limit_bytes=4 << 20),
    )(keep, swap_core(give))
    return [parts[0]] + [
        send(parts[k], lambda x, z, y, c: (x, z, y ^ k, c)) for k in (1, 2, 3)
    ]


def in_order(parts):
    y = place()[2]
    parts = [part[...] for part in parts]
    return jnp.concatenate([pick(parts, y ^ v) for v in range(4)], 0)


def root_columns(every):
    def body(every, keep, give):
        first = place()[3] == 0
        for v in range(4):
            for half in range(2):
                here = slice(768 * half, 768 * (half + 1))
                own, other = every[4 * v + half], every[4 * v + 2 + half]
                keep[v, :, here] = jnp.where(first, own, other)
                give[v, :, here] = jnp.where(first, other, own)

    block = pl.BlockSpec(memory_space=pltpu.VMEM)
    return to_columns(
        *pl.pallas_call(
            body,
            name="root_columns",
            out_shape=[jax.ShapeDtypeStruct((4, 8, 1536), jnp.float32)] * 2,
            in_specs=[block],
            out_specs=[block] * 2,
            compiler_params=pltpu.CompilerParams(vmem_limit_bytes=4 << 20),
        )(every)
    )


def bound_columns(root, middle):
    def body(root, middle, keep, give):
        x, z, y, c = place()

        def piece(number):
            here = slice(128 * (number % 6), 128 * (number % 6 + 1))
            if number < 48:
                return jnp.where(x % 2 == 1, root[8 + number // 6, :, here], root[number // 6, :, here])
            number -= 48
            return middle[number // 4, :, 128 * (number % 4) : 128 * (number % 4 + 1)]

        for v in range(4):
            for k in range(10):
                here = slice(128 * k, 128 * (k + 1))
                own, other = piece(20 * v + k), piece(20 * v + 10 + k)
                keep[v, :, here] = jnp.where(c == 0, own, other)
                give[v, :, here] = jnp.where(c == 0, other, own)

    block = pl.BlockSpec(memory_space=pltpu.VMEM)
    return to_columns(
        *pl.pallas_call(
            body,
            name="bound_columns",
            out_shape=[jax.ShapeDtypeStruct((4, 8, 1280), jnp.float32)] * 2,
            in_specs=[block] * 2,
            out_specs=[block] * 2,
            compiler_params=pltpu.CompilerParams(vmem_limit_bytes=4 << 20),
        )(root, middle)
    )


def root_product(parts, operator):
    def vectors(parts):
        lines = [jnp.concatenate([parts[12 * k + n] for n in range(12)], 1) for k in range(8)]
        return jnp.concatenate(lines, 0)

    def store(number, tile, parts, keep, give):
        shared(tile, slice(256 * number, 256 * (number + 1)), keep, give)

    return product("root", vectors, operator, [parts], [(4, 8, 768)] * 2, store, 256)


def middle_product(parts, operator, added):
    def vectors(*refs):
        return in_order(refs[:4])

    def store(number, tile, *refs):
        here = slice(256 * number, 256 * (number + 1))
        shared(tile + refs[4][:, here], here, *refs[-2:])

    shapes = [(4, 8, 512)] * 2
    return product("middle", vectors, operator, [*parts, added], shapes, store, 256)


def split_ahead(operator):
    def body(held, over, under):
        for number in range(4):
            here = slice(256 * number, 256 * (number + 1))
            over[here, :], under[here, :] = halves(held[here, :])

    return pl.pallas_call(
        body,
        name="split_ahead",
        out_shape=[jax.ShapeDtypeStruct(operator.shape, jnp.bfloat16)] * 2,
        in_specs=[pl.BlockSpec(memory_space=pltpu.VMEM)],
        out_specs=[pl.BlockSpec(memory_space=pltpu.VMEM)] * 2,
        compiler_params=pltpu.CompilerParams(vmem_limit_bytes=4 << 20),
    )(operator)


def last_product(bound, over, under, added):
    def body(*refs):
        added, over, under, keep, give = refs[4:]
        high, low = halves(in_order(refs[:4]))
        both = jnp.concatenate([high, low], 0)
        for number in range(4):
            here = slice(256 * number, 256 * (number + 1))
            first = lax.dot_general(both, over[here, :], ROWS, preferred_element_type=jnp.float32)
            second = lax.dot_general(high, under[here, :], ROWS, preferred_element_type=jnp.float32)
            tile = first[:64] + (first[64:] + second) + added[:, here]
            shared(tile, here, keep, give)

    return pl.pallas_call(
        body,
        name="low_solve",
        out_shape=[jax.ShapeDtypeStruct((4, 8, 1024), jnp.float32)] * 2,
        in_specs=[pl.BlockSpec(memory_space=pltpu.VMEM)] * 7,
        out_specs=[pl.BlockSpec(memory_space=pltpu.VMEM)] * 2,
        compiler_params=pltpu.CompilerParams(vmem_limit_bytes=4 << 20),
    )(*bound, added, over, under)


def local(
    particular, root_inverse, mid_inverse, low_inverse, mid_lift, low_lift, mid_solve, low_solve
):
    x, z, y, c = place()
    xh, xl = x // 2, x % 2

    inner = particular[:, 512:].reshape(8, 4, 2, 512)
    keep = lax.dynamic_index_in_dim(inner, c, 2, False).transpose(1, 0, 2)
    got = swap_core(lax.dynamic_index_in_dim(inner, 1 - c, 2, False).transpose(1, 0, 2))
    both = jnp.concatenate([jnp.where(c == 0, keep, got), jnp.where(c == 0, got, keep)], 1)
    jump_two = over_zy(copies(both, 4).reshape(16, 16, 512))

    low_part, keep, give = low_product(jump_two, low_inverse)
    half = added(keep, swap_core(give))
    blocks = [half] + [send(half, lambda x, z, y, c: (x, z ^ k, y, c)) for k in (1, 2, 3)]
    blocks = list(turned(blocks))
    low_w = blocks[:1] + [
        send(blocks[k], lambda x, z, y, c: (x, z, y ^ k, c)) for k in (1, 2, 3)
    ]

    keep, give, mine, other = lift_product(low_w, particular, low_lift)

    blocks = added(keep, swap_core(give)).reshape(32, 8, 512)
    blocks, other, apart = lax.optimization_barrier((blocks, other, particular))
    jump_one = over_half(gathered(over_low(blocks), 8)[1])

    mid_part = mid_product(jump_one, mid_inverse)
    mid_sum = sum_y(mid_part + swap_core(mid_part))
    mid_w = send(
        mid_sum, lambda x, z, y, c: (x // 2 * 2 + c, y ^ z, x % 2 * 2 + z // 2, z % 2)
    )

    here = (jnp.arange(4) == y)[:, None, None]
    nothing = jnp.zeros((8, 2048), jnp.float32)
    outer = jnp.where(
        z == 1, jnp.concatenate([nothing, apart[:, :512]], 1), apart[:, :2560]
    )
    outer_half = mine + swap_core(other) + jnp.where(here, outer[None], 0.0)
    beyond = jnp.where(here, apart[None, :, 2560:3072], 0.0)
    next_z = send(
        pick(
            [
                jnp.concatenate([beyond, outer_half[:, :, 1536:]], 2),
                outer_half[:, :, 512:2048],
                outer_half[:, :, :1536],
            ],
            z,
        ),
        lambda x, z, y, c: (x, z + 1, y, c) if z < 3 else None,
    )
    thirds = apart[:, 3072:].reshape(8, 3, 512).transpose(1, 0, 2)
    far_z = send(
        jnp.where(
            z == 0,
            jnp.concatenate([thirds, jnp.zeros((1, 8, 512), jnp.float32)], 0),
            outer_half[:, :, 2048:],
        ),
        lambda x, z, y, c: (x, z + 2, y, c) if z < 2 else None,
    )
    wide = jnp.concatenate([far_z[0], far_z[1], far_z[2]], 1)
    outer_one = pick(
        [
            outer_half[:, :, :1536],
            jnp.concatenate([next_z[:, :, 512:], outer_half[:, :, :512] + next_z[:, :, :512]], 2),
            next_z + jnp.where(here, wide[None], 0.0),
            jnp.concatenate([far_z, next_z[:, :, :1024]], 2),
        ],
        z,
    )

    shares = mid_lift_product(mid_w, outer_one, mid_lift)
    root_jump = over_all(mixed(over_all(shares)))

    root_part = root_product(root_jump, root_inverse)
    root_values, root_every = gathered(over_columns(*root_part), 16)
    root_every = over_leaf(root_every)
    root_block = root_columns(root_every)

    middle_part = middle_product(root_block, mid_solve, mid_part)
    middle_values, middle_every = gathered(over_columns(*middle_part), 8)
    middle_every, low_solve = lax.optimization_barrier((middle_every, low_solve))
    middle_every = over_half(middle_every)
    over, under = split_ahead(low_solve)

    bound = bound_columns(root_every, middle_every)
    lower_values = total(over_columns(*last_product(bound, over, under, low_part)))
    return (root_values, middle_values, lower_values)


def solution(mesh):
    placed = (P("blk", "leaf"),) + (P("leaf", "blk"),) * 7
    return jax.shard_map(
        local,
        mesh=mesh,
        in_specs=placed,
        out_specs=(P("blk", "leaf"),) * 3,
        check_vma=False,
    )
```

```python
import jax
import jax.numpy as jnp
from jax import lax
from jax.experimental import pallas as pl
from jax.experimental.pallas import tpu as pltpu
from jax.sharding import PartitionSpec as P

AXES = ("leaf", "blk")
DEVICES = [(s // 32, s // 8 % 4, s // 2 % 4, s % 2) for s in range(128)]
ROWS = (((1,), (1,)), ((), ()))


def flat(x, z, y, c):
    return ((x * 4 + z) * 4 + y) * 2 + c


def send(value, hop):
    pairs = []
    for source, place in enumerate(DEVICES):
        target = hop(*place)
        if target is not None:
            pairs.append((source, flat(*target)))
    return lax.ppermute(value, AXES, pairs)


def exchange(value, key, order):
    groups = {}
    for source, place in enumerate(DEVICES):
        groups.setdefault(key(*place), []).append((order(*place), source))
    members = [[source for _, source in sorted(group)] for group in groups.values()]
    return lax.all_to_all(value, AXES, 0, 0, axis_index_groups=members)


def over_blk(value):
    return exchange(value, lambda x, z, y, c: (x, z), lambda x, z, y, c: 2 * y + c)


def over_leaf(value):
    return exchange(value, lambda x, z, y, c: (y, c), lambda x, z, y, c: 4 * x + z)


def over_half(value):
    return exchange(value, lambda x, z, y, c: (x // 2, y, c), lambda x, z, y, c: 4 * x + z)


def over_low(value):
    return exchange(value, lambda x, z, y, c: (x // 2, c), lambda x, z, y, c: (x, z, y))


def over_plane(value):
    return exchange(value, lambda x, z, y, c: x, lambda x, z, y, c: (z, y, c))


def over_all(value):
    return exchange(value, lambda x, z, y, c: 0, flat)


def copies(value, number):
    return jnp.broadcast_to(value[None], (number, *value.shape))


def swap_core(value):
    return send(value, lambda x, z, y, c: (x, z, y, 1 - c))


def sum_y(value):
    return value + total([send(value, lambda x, z, y, c: (x, z, y ^ k, c)) for k in (1, 2, 3)])


def cols(value, start, size):
    return lax.dynamic_slice_in_dim(value, start, size, value.ndim - 1)


def pick(pieces, index):
    out = pieces[0]
    for number in range(1, len(pieces)):
        out = jnp.where(index == number, pieces[number], out)
    return out


def total(parts):
    out = parts[0]
    for part in parts[1:]:
        out = out + part
    return out


def place():
    leaf, blk = lax.axis_index("leaf"), lax.axis_index("blk")
    return leaf // 4, leaf % 4, blk // 2, blk % 2


def halves(value):
    high = value.astype(jnp.bfloat16)
    return high, (value - high.astype(jnp.float32)).astype(jnp.bfloat16)


def product(name, vectors, operator, inputs, outputs, store, tile, fetch=0):
    height, depth = operator.shape
    count, steps = len(inputs), height // tile

    def body(*refs):
        given, held, results = refs[:count], refs[count], refs[count + 1 :]
        moves = []
        if fetch:
            *results, room, sems = results
            for number in range(steps):
                here = pl.ds(number * tile, tile)
                moves.append(pltpu.make_async_copy(held.at[here], room.at[here], sems.at[number]))
                moves[-1].start()
            held = room
        high, low = halves(vectors(*given))
        both = jnp.concatenate([high, low], 0)
        for number in range(steps):
            if fetch:
                moves[number].wait()
            over, under = halves(held[number * tile : (number + 1) * tile, :])
            first = lax.dot_general(both, over, ROWS, preferred_element_type=jnp.float32)
            second = lax.dot_general(high, under, ROWS, preferred_element_type=jnp.float32)
            store(number, first[:64] + (first[64:] + second), *given, *results)

    block = pl.BlockSpec(memory_space=pltpu.VMEM)
    return pl.pallas_call(
        body,
        name=name,
        out_shape=[jax.ShapeDtypeStruct(shape, jnp.float32) for shape in outputs],
        in_specs=[block] * count + [pl.BlockSpec(memory_space=pl.ANY) if fetch else block],
        out_specs=[block] * len(outputs),
        scratch_shapes=[
            pltpu.VMEM((height, depth), jnp.float32),
            pltpu.SemaphoreType.DMA((steps,)),
        ]
        if fetch
        else [],
        compiler_params=pltpu.CompilerParams(vmem_limit_bytes=(fetch or 4) << 20),
        cost_estimate=pl.CostEstimate(
            flops=6 * 64 * height * depth, bytes_accessed=4 * height * depth, transcendentals=0
        ),
    )(*inputs, operator)


def gathered(parts, number):
    parts = parts if isinstance(parts, list) else [parts]
    count = len(parts)

    def body(*refs):
        value, every = refs[count:]
        if count == 1:
            summed = total([refs[0][k] for k in range(refs[0].shape[0])])
        else:
            summed = total([ref[...] for ref in refs[:count]])
        value[...] = summed
        for k in range(number):
            every[k] = summed

    shape = parts[0].shape[1:] if count == 1 else parts[0].shape
    block = pl.BlockSpec(memory_space=pltpu.VMEM)
    return pl.pallas_call(
        body,
        name="gathered",
        out_shape=[
            jax.ShapeDtypeStruct(shape, jnp.float32),
            jax.ShapeDtypeStruct((number, *shape), jnp.float32),
        ],
        in_specs=[block] * count,
        out_specs=[block] * 2,
        compiler_params=pltpu.CompilerParams(vmem_limit_bytes=4 << 20),
    )(*parts)


def added(first, second, number=None):
    def body(first, second, out):
        if number is None:
            out[...] = first[...] + second[...]
        else:
            summed = first[...] + second[...]
            for k in range(number):
                out[k] = summed

    shape = first.shape if number is None else (number, *first.shape)
    return pl.pallas_call(
        body,
        name="added",
        out_shape=jax.ShapeDtypeStruct(shape, jnp.float32),
        in_specs=[pl.BlockSpec(memory_space=pltpu.VMEM)] * 2,
        out_specs=pl.BlockSpec(memory_space=pltpu.VMEM),
        compiler_params=pltpu.CompilerParams(vmem_limit_bytes=4 << 20),
    )(first, second)


def fanned(particular):
    def body(particular, out):
        for block in range(8):
            piece = particular[:, 512 + 512 * block : 1024 + 512 * block]
            for k in range(4):
                out[8 * k + block] = piece

    return pl.pallas_call(
        body,
        name="fanned",
        out_shape=jax.ShapeDtypeStruct((32, 8, 512), jnp.float32),
        in_specs=[pl.BlockSpec(memory_space=pltpu.VMEM)],
        out_specs=pl.BlockSpec(memory_space=pltpu.VMEM),
        compiler_params=pltpu.CompilerParams(vmem_limit_bytes=4 << 20),
    )(particular)


def low_product(jump, operator):
    def vectors(jump):
        return (jump[24:32] - jump[8:16]).reshape(64, 512)

    def store(number, tile, jump, part, keep, give):
        part[:, 512 * number : 512 * (number + 1)] = tile
        mine = place()[3] == number
        keep[...] = jnp.where(mine, tile, keep[...])
        give[...] = jnp.where(mine, give[...], tile)

    shapes = [(64, 1024), (64, 512), (64, 512)]
    return product("low_w", vectors, operator, [jump], shapes, store, 512)


def turned(parts):
    def body(*refs):
        x, z, y, c = place()
        for shift in range(4):

            @pl.when(z ^ y == shift)
            def _():
                for k in range(4):
                    refs[4 + k][...] = refs[shift ^ k][...]

    block = pl.BlockSpec(memory_space=pltpu.VMEM)
    return pl.pallas_call(
        body,
        name="turned",
        out_shape=[jax.ShapeDtypeStruct(parts[0].shape, jnp.float32)] * 4,
        in_specs=[block] * 4,
        out_specs=[block] * 4,
        compiler_params=pltpu.CompilerParams(vmem_limit_bytes=4 << 20),
    )(*parts)


def lift_product(parts, particular, operator):
    def vectors(*refs):
        return refs[0][...] + refs[1][...] + (refs[2][...] + refs[3][...])

    def store(number, tile, *refs):
        particular, keep, give, mine, other = refs[4:]
        x, z, y, c = place()
        sign = jnp.where(x % 2 == 1, 1.0, -1.0)
        if number == 0:
            keep[...] = jnp.zeros(keep.shape, jnp.float32)
            give[...] = jnp.zeros(give.shape, jnp.float32)
            for block in range(8):
                v, core = block // 2, block % 2
                source = 1024 + 512 * block if block < 7 else 0

                @pl.when((z == (2 if block < 7 else 3)) & (c == core))
                def _():
                    keep[2 * y + c, v] = sign * particular[:, source : source + 512]

                @pl.when((z == (2 if block < 7 else 3)) & (c != core))
                def _():
                    give[2 * y + c, v] = sign * particular[:, source : source + 512]

        here = pl.ds(512 * number, 512)
        block = number + jnp.where(z == 3, 3, -2)
        valid = (z == 3) | ((z == 2) & (number >= 2))
        row = jnp.clip(block // 2, 0, 3)

        @pl.when(valid & (block % 2 == c))
        def _():
            for k in range(8):
                keep[k, row] += sign * tile[8 * k : 8 * k + 8]

        @pl.when(valid & (block % 2 != c))
        def _():
            for k in range(8):
                give[k, row] += sign * tile[8 * k : 8 * k + 8]

        shared(tile, here, mine, other)

    shapes = [(8, 4, 8, 512)] * 2 + [(4, 8, 2560)] * 2
    return product(
        "low_lift", vectors, operator, [*parts, particular], shapes, store, 512
    )


def mid_product(parts, operator):
    def vectors(parts):
        return parts[...].reshape(64, 512)

    def store(number, tile, parts, out):
        out[:, 256 * number : 256 * (number + 1)] = tile

    return product("mid_w", vectors, operator, [parts], [(64, 512)], store, 256)[0]


def mid_lift_product(mid_w, outer, operator):
    def vectors(mid_w, outer):
        return mid_w[...]

    def store(number, tile, mid_w, outer, out):
        x, z, y, c = place()
        if number == 0:
            out[96:] = jnp.zeros((32, 8, 128), jnp.float32)
        added = outer[:, :, 256 * number : 256 * (number + 1)]
        sign = jnp.where(x // 2 == 1, 1.0, -1.0)
        pairs = tile.reshape(4, 2, 8, 256)
        for core in range(2):
            whole = sign * (pairs[:, core] + jnp.where(c == core, added, 0.0))
            for v in range(4):
                first = 12 * (2 * v + core) + 2 * number
                out[first] = whole[v, :, :128]
                out[first + 1] = whole[v, :, 128:]

    return product(
        "mid_lift", vectors, operator, [mid_w, outer], [(128, 8, 128)], store, 256
    )[0]


def mixed(parts):
    def body(parts, out):
        for block in range(8):
            given = [parts[64 * side + 8 * block + k] for side in range(2) for k in range(8)]
            summed = total(given)
            for leaf in range(16):
                out[8 * leaf + block] = summed

    return pl.pallas_call(
        body,
        name="mixed",
        out_shape=jax.ShapeDtypeStruct((128, 8, 128), jnp.float32),
        in_specs=[pl.BlockSpec(memory_space=pltpu.VMEM)],
        out_specs=pl.BlockSpec(memory_space=pltpu.VMEM),
        compiler_params=pltpu.CompilerParams(vmem_limit_bytes=4 << 20),
    )(parts)


def shared(tile, here, keep, give):
    first = place()[3] == 0
    pairs = tile.reshape(4, 2, 8, tile.shape[1])
    keep[:, :, here] = jnp.where(first, pairs[:, 0], pairs[:, 1])
    give[:, :, here] = jnp.where(first, pairs[:, 1], pairs[:, 0])


def over_columns(keep, give):
    def body(keep, got, *out):
        y = place()[2]
        for mine in range(4):

            @pl.when(y == mine)
            def _():
                for k in range(4):
                    out[k][...] = keep[mine ^ k] + got[mine ^ k]

    block = pl.BlockSpec(memory_space=pltpu.VMEM)
    parts = pl.pallas_call(
        body,
        name="over_columns",
        out_shape=[jax.ShapeDtypeStruct(keep.shape[1:], jnp.float32)] * 4,
        in_specs=[block] * 2,
        out_specs=[block] * 4,
        compiler_params=pltpu.CompilerParams(vmem_limit_bytes=4 << 20),
    )(keep, swap_core(give))
    return [parts[0]] + [
        send(parts[k], lambda x, z, y, c: (x, z, y ^ k, c)) for k in (1, 2, 3)
    ]


def to_columns(keep, give):
    def body(keep, got, *out):
        x, z, y, c = place()
        for mine in range(4):

            @pl.when(y == mine)
            def _():
                for k in range(4):
                    own, other = keep[mine ^ k], got[mine ^ k]
                    out[k][0:8] = jnp.where(c == 0, own, other)
                    out[k][8:16] = jnp.where(c == 0, other, own)

    block = pl.BlockSpec(memory_space=pltpu.VMEM)
    parts = pl.pallas_call(
        body,
        name="to_columns",
        out_shape=[jax.ShapeDtypeStruct((16, keep.shape[2]), jnp.float32)] * 4,
        in_specs=[block] * 2,
        out_specs=[block] * 4,
        compiler_params=pltpu.CompilerParams(vmem_limit_bytes=4 << 20),
    )(keep, swap_core(give))
    return [parts[0]] + [
        send(parts[k], lambda x, z, y, c: (x, z, y ^ k, c)) for k in (1, 2, 3)
    ]


def in_order(parts):
    y = place()[2]
    parts = [part[...] for part in parts]
    return jnp.concatenate([pick(parts, y ^ v) for v in range(4)], 0)


def root_columns(every):
    def body(every, keep, give):
        first = place()[3] == 0
        for v in range(4):
            for half in range(2):
                here = slice(768 * half, 768 * (half + 1))
                own, other = every[4 * v + half], every[4 * v + 2 + half]
                keep[v, :, here] = jnp.where(first, own, other)
                give[v, :, here] = jnp.where(first, other, own)

    block = pl.BlockSpec(memory_space=pltpu.VMEM)
    return to_columns(
        *pl.pallas_call(
            body,
            name="root_columns",
            out_shape=[jax.ShapeDtypeStruct((4, 8, 1536), jnp.float32)] * 2,
            in_specs=[block],
            out_specs=[block] * 2,
            compiler_params=pltpu.CompilerParams(vmem_limit_bytes=4 << 20),
        )(every)
    )


def bound_columns(root, middle):
    def body(root, middle, keep, give):
        x, z, y, c = place()

        def piece(number):
            here = slice(128 * (number % 6), 128 * (number % 6 + 1))
            if number < 48:
                return jnp.where(x % 2 == 1, root[8 + number // 6, :, here], root[number // 6, :, here])
            number -= 48
            return middle[number // 4, :, 128 * (number % 4) : 128 * (number % 4 + 1)]

        for v in range(4):
            for k in range(10):
                here = slice(128 * k, 128 * (k + 1))
                own, other = piece(20 * v + k), piece(20 * v + 10 + k)
                keep[v, :, here] = jnp.where(c == 0, own, other)
                give[v, :, here] = jnp.where(c == 0, other, own)

    block = pl.BlockSpec(memory_space=pltpu.VMEM)
    return to_columns(
        *pl.pallas_call(
            body,
            name="bound_columns",
            out_shape=[jax.ShapeDtypeStruct((4, 8, 1280), jnp.float32)] * 2,
            in_specs=[block] * 2,
            out_specs=[block] * 2,
            compiler_params=pltpu.CompilerParams(vmem_limit_bytes=4 << 20),
        )(root, middle)
    )


def root_product(parts, operator):
    def vectors(parts):
        lines = [jnp.concatenate([parts[12 * k + n] for n in range(12)], 1) for k in range(8)]
        return jnp.concatenate(lines, 0)

    def store(number, tile, parts, keep, give):
        shared(tile, slice(256 * number, 256 * (number + 1)), keep, give)

    return product("root", vectors, operator, [parts], [(4, 8, 768)] * 2, store, 256)


def middle_product(parts, operator, added):
    def vectors(*refs):
        return in_order(refs[:4])

    def store(number, tile, *refs):
        here = slice(256 * number, 256 * (number + 1))
        shared(tile + refs[4][:, here], here, *refs[-2:])

    shapes = [(4, 8, 512)] * 2
    return product("middle", vectors, operator, [*parts, added], shapes, store, 256)


def split_ahead(operator):
    def body(held, over, under):
        for number in range(4):
            here = slice(256 * number, 256 * (number + 1))
            over[here, :], under[here, :] = halves(held[here, :])

    return pl.pallas_call(
        body,
        name="split_ahead",
        out_shape=[jax.ShapeDtypeStruct(operator.shape, jnp.bfloat16)] * 2,
        in_specs=[pl.BlockSpec(memory_space=pltpu.VMEM)],
        out_specs=[pl.BlockSpec(memory_space=pltpu.VMEM)] * 2,
        compiler_params=pltpu.CompilerParams(vmem_limit_bytes=4 << 20),
    )(operator)


def last_product(bound, over, under, added):
    def body(*refs):
        added, over, under, keep, give = refs[4:]
        high, low = halves(in_order(refs[:4]))
        both = jnp.concatenate([high, low], 0)
        for number in range(4):
            here = slice(256 * number, 256 * (number + 1))
            first = lax.dot_general(both, over[here, :], ROWS, preferred_element_type=jnp.float32)
            second = lax.dot_general(high, under[here, :], ROWS, preferred_element_type=jnp.float32)
            tile = first[:64] + (first[64:] + second) + added[:, here]
            shared(tile, here, keep, give)

    return pl.pallas_call(
        body,
        name="low_solve",
        out_shape=[jax.ShapeDtypeStruct((4, 8, 1024), jnp.float32)] * 2,
        in_specs=[pl.BlockSpec(memory_space=pltpu.VMEM)] * 7,
        out_specs=[pl.BlockSpec(memory_space=pltpu.VMEM)] * 2,
        compiler_params=pltpu.CompilerParams(vmem_limit_bytes=4 << 20),
    )(*bound, added, over, under)


def local(
    particular, root_inverse, mid_inverse, low_inverse, mid_lift, low_lift, mid_solve, low_solve
):
    x, z, y, c = place()
    xh, xl = x // 2, x % 2

    jump_two = over_plane(fanned(particular))

    low_part, keep, give = low_product(jump_two, low_inverse)
    half = added(keep, swap_core(give))
    blocks = [half] + [send(half, lambda x, z, y, c: (x, z ^ k, y, c)) for k in (1, 2, 3)]
    blocks = list(turned(blocks))
    low_w = blocks[:1] + [
        send(blocks[k], lambda x, z, y, c: (x, z, y ^ k, c)) for k in (1, 2, 3)
    ]

    keep, give, mine, other = lift_product(low_w, particular, low_lift)

    blocks = added(keep, swap_core(give)).reshape(32, 8, 512)
    blocks, other, apart = lax.optimization_barrier((blocks, other, particular))
    jump_one = over_half(gathered(over_low(blocks), 8)[1])

    mid_part = mid_product(jump_one, mid_inverse)
    mid_sum = sum_y(mid_part + swap_core(mid_part))
    mid_w = send(
        mid_sum, lambda x, z, y, c: (x // 2 * 2 + c, y ^ z, x % 2 * 2 + z // 2, z % 2)
    )

    here = (jnp.arange(4) == y)[:, None, None]
    nothing = jnp.zeros((8, 2048), jnp.float32)
    outer = jnp.where(
        z == 1, jnp.concatenate([nothing, apart[:, :512]], 1), apart[:, :2560]
    )
    outer_half = mine + swap_core(other) + jnp.where(here, outer[None], 0.0)
    beyond = jnp.where(here, apart[None, :, 2560:3072], 0.0)
    next_z = send(
        pick(
            [
                jnp.concatenate([beyond, outer_half[:, :, 1536:]], 2),
                outer_half[:, :, 512:2048],
                outer_half[:, :, :1536],
            ],
            z,
        ),
        lambda x, z, y, c: (x, z + 1, y, c) if z < 3 else None,
    )
    thirds = apart[:, 3072:].reshape(8, 3, 512).transpose(1, 0, 2)
    far_z = send(
        jnp.where(
            z == 0,
            jnp.concatenate([thirds, jnp.zeros((1, 8, 512), jnp.float32)], 0),
            outer_half[:, :, 2048:],
        ),
        lambda x, z, y, c: (x, z + 2, y, c) if z < 2 else None,
    )
    wide = jnp.concatenate([far_z[0], far_z[1], far_z[2]], 1)
    outer_one = pick(
        [
            outer_half[:, :, :1536],
            jnp.concatenate([next_z[:, :, 512:], outer_half[:, :, :512] + next_z[:, :, :512]], 2),
            next_z + jnp.where(here, wide[None], 0.0),
            jnp.concatenate([far_z, next_z[:, :, :1024]], 2),
        ],
        z,
    )

    shares = mid_lift_product(mid_w, outer_one, mid_lift)
    root_jump = over_all(mixed(over_all(shares)))

    root_part = root_product(root_jump, root_inverse)
    root_values, root_every = gathered(over_columns(*root_part), 16)
    root_every = over_leaf(root_every)
    root_block = root_columns(root_every)

    middle_part = middle_product(root_block, mid_solve, mid_part)
    middle_values, middle_every = gathered(over_columns(*middle_part), 8)
    middle_every, low_solve = lax.optimization_barrier((middle_every, low_solve))
    middle_every = over_half(middle_every)
    over, under = split_ahead(low_solve)

    bound = bound_columns(root_every, middle_every)
    lower_values = total(over_columns(*last_product(bound, over, under, low_part)))
    return (root_values, middle_values, lower_values)


def solution(mesh):
    placed = (P("blk", "leaf"),) + (P("leaf", "blk"),) * 7
    return jax.shard_map(
        local,
        mesh=mesh,
        in_specs=placed,
        out_specs=(P("blk", "leaf"),) * 3,
        check_vma=False,
    )
```
